128 devices in a mesh: lon: 32 (over x, y, z_lo), lat: 4 (over z_hi, core).
Axes of the slice: x: 4, y: 4, z: 4 (z_hi: 2, z_lo: 2; z = z_hi * 2 + z_lo), core: 2. Of those that a mesh axis runs over, the one named last changes fastest.
Arguments:
- state: bfloat16 [512, 3, 16, 4096], P('lat', None, None, 'lon'), may hold values from -6 to 6
- weights: bfloat16 [512, 128, 4096], P('lat', None, 'lon'), may hold values from -1.767767 to 1.767767
- owners: int32 [32, 512, 1], P('lon', 'lat'), may hold values from 0 to 127; in each aligned block of 128 rows (0 to 127, 128 to 255, ..., all dimensions but the last counted through in order) at most 2 rows name the same one
- source_rows: int32 [32, 512], P('lon', 'lat'), may hold values from 0 to 127
- cutoffs: int32 [32], replicated, may hold values from 1 to 1023
- stiffness: float32 [512, 16, 4096], P('lat', None, 'lon'), may hold values from 0.02 to 1
Outputs:
- updated: float32 [512, 3, 16, 4096], P('lat', None, None, 'lon')
The draws below stay inside these ranges and needn't reach their ends.
Inputs may be any that keep to these rules, and one draw needn't show every extreme that they name: `owners`: device d is longitude block d // 4 and latitude band d % 4; among the 128 target blocks of one device no device is named more than 2 times, and some device is named exactly 2 times.
All inputs are finite; a program needn't handle non-finite values.
Results may differ from the reference program's by a relative error of at most 0.0003.
Values may be sent and summed in bfloat16 or wider, within the bound.
No kernel may reach another device: no remote copies, remote signals or barrier semaphores. Data moves between devices by JAX's collectives and lax.ppermute only.
A program may use at most 128 MiB of HBM per device.

```python
import math
import jax
import jax.numpy as jnp
import numpy as np
from jax import lax

LON_DEV = 128
LAT_DEV = 128
LEV = 16
ITERS = 5
NLAT = 512
NLON = 4096
MODES = 1024
POLAR = 16
CAP = 2
N_LON = 32
N_LAT = 4
DEVICES = 128


def draw_cutoffs(key, part):
    key = jax.random.fold_in(key, 7)
    position = jnp.arange(2 * POLAR, dtype=jnp.int32)
    distance = jnp.where(position < POLAR, position, 2 * POLAR - 1 - position)
    base = 1 + distance * (MODES - 2) // (POLAR - 1)
    jitter = jax.random.randint(key, (2 * POLAR,), -3, 4, dtype=jnp.int32)
    inner = (distance > 0) & (distance < POLAR - 1)
    return jnp.clip(base + jnp.where(inner, jitter, 0), 1, MODES - 1).astype(jnp.int32)


def rising_scale():
    rows = jnp.arange(NLAT, dtype=jnp.float32) / NLAT
    columns = jnp.arange(NLON, dtype=jnp.float32) / NLON
    exponent = rows[:, None, None] + columns[None, None, :] - 1.0
    return jnp.exp(exponent * jnp.log(3.0))


def device_levels(key, lowest, highest):
    table = jax.random.uniform(key, (N_LAT, N_LON), jnp.float32, lowest, highest)
    band = jnp.arange(NLAT, dtype=jnp.int32) // LAT_DEV
    block = jnp.arange(NLON, dtype=jnp.int32) // LON_DEV
    return table[band][:, block]


def draw_weights(key, part):
    key = jax.random.fold_in(key, 11)
    value_key, level_key = jax.random.split(key)
    values = jnp.clip(jax.random.normal(value_key, (NLAT, LON_DEV, NLON), jnp.float32), -4.0, 4.0)
    factor = rising_scale()
    level = jnp.exp(device_levels(level_key, -1.6, 0.4))
    return (values * factor * level[:, None, :] * LON_DEV ** (-0.5)).astype(jnp.bfloat16)


def draw_stiffness(key, part):
    key = jax.random.fold_in(key, 13)
    level_key, cell_key = jax.random.split(key)
    lowest = jnp.log(0.02)
    centers = device_levels(level_key, lowest, 0.0)
    jitter = jnp.clip(jax.random.normal(cell_key, (NLAT, LEV, NLON), jnp.float32), -2.0, 2.0) * 0.35
    exponent = jnp.clip(centers[:, None, :] + jitter, lowest, 0.0)
    return jnp.exp(exponent).astype(jnp.float32)


def plant(values, rng, low, high):
    longest = values.shape.index(max(values.shape))
    spots = []
    for shift in (0, 1):
        where = [jax.random.randint(jax.random.fold_in(rng, axis), (), 0, length) for axis, length in enumerate(values.shape)]
        where[longest] = (where[longest] + shift) % values.shape[longest]
        spots.append(tuple(where))
    return values.at[spots[0]].set(low).at[spots[1]].set(high)


def level_of(own_key, shape, shards, smallest, largest):
    loudness = 1.0
    for dim, blocks in shards:
        steps = jax.random.uniform(jax.random.fold_in(jax.random.fold_in(own_key, 6), dim), (blocks,), jnp.float32, smallest / len(shards), largest / len(shards))
        loudness = loudness * jnp.repeat(jnp.exp(steps), shape[dim] // blocks).reshape((-1,) + (1,) * (len(shape) - 1 - dim))
    return loudness


def routed_block(rng, own, number, rows, number_of, top, most, lean):
    sequence = jax.random.permutation(rng, number_of)
    heavy_load, usual = load_shares(number_of, rows * top, most, lean, True), load_shares(number_of, rows * top, most, lean, False)
    places = jnp.arange(number_of)

    def named(lengths, rotation):
        used = int((lengths > 0).sum())
        fixed = max(1, used // 4)
        moved = fixed + (places - fixed + rotation * (used - fixed)) % max(1, number_of - fixed)
        return jnp.zeros((number_of,), jnp.int32).at[sequence[jnp.where(places < fixed, places, moved)]].set(jnp.asarray(lengths, jnp.int32))

    lengths = jnp.where(number % 4 == 0, named(heavy_load, number // 4), named(usual, number - number // 4 - 1))
    mixed = jax.random.permutation(jax.random.fold_in(own, 3), number_of)
    donor, sink = mixed[0:number_of // 2 * 2:2], mixed[1:number_of // 2 * 2:2]
    room = jnp.minimum(lengths[donor] - 1, most - lengths[sink]) // 2
    room = jnp.where((donor == sequence[0]) | (sink == sequence[0]) | (lengths[sink] == 0), 0, jnp.maximum(room, 0))
    moved = jax.random.randint(jax.random.fold_in(own, 4), (number_of // 2,), 0, 1 << 20) % (room + 1)
    lengths = lengths.at[donor].add(-moved).at[sink].add(moved)
    items = jnp.searchsorted(jnp.cumsum(lengths), jnp.arange(rows * top), side="right").astype(jnp.int32)
    table = items.reshape(top, rows).T
    table = table[jax.random.permutation(jax.random.fold_in(own, 1), rows)]
    rotation = jax.random.randint(jax.random.fold_in(own, 2), (rows, 1), 0, top)
    return jnp.take_along_axis(table, (jnp.arange(top)[None, :] + rotation) % top, axis=1)


def load_shares(number_of, total, bound, lean, full):
    loads = [(1 << 20) // math.isqrt(rank ** lean) + 1 for rank in range(1, number_of + 1)]
    largest = bound if full else min(bound, max(-(-total // number_of), total * loads[0] // sum(loads)))
    least = 1 if total - largest >= number_of - 1 else 0
    given, surplus = [largest] + [least] * (number_of - 1), total - largest - least * (number_of - 1)
    while surplus > 0:
        candidates = [i for i in range(1, number_of) if given[i] < largest] or [i for i in range(1, number_of) if given[i] < bound]
        whole, remaining = sum([loads[i] for i in candidates]), surplus
        for i in candidates:
            addition = min(bound - given[i], max(1, remaining * loads[i] // whole), surplus)
            given[i] = given[i] + addition
            surplus = surplus - addition
    return np.array(given)


def scatter_about(key, extent, width, most, cuts=(), kind=jnp.bfloat16):
    drawn = jax.random.normal(key, extent, jnp.float32) * width
    if len(cuts) > 0:
        drawn = level_of(key, extent, cuts, -0.22, 0.18) * drawn
    return jnp.clip(drawn, min=-most, max=most).astype(kind)


def setup_inputs(seed: int = 0) -> dict:
    keys = jax.random.split(jax.random.key(seed), 7)
    state = scatter_about(keys[0], (NLAT, 3, LEV, NLON), 1.0, 6.0, ((0, 4), (3, 32)))
    weights = draw_weights(jax.random.fold_in(keys[6], 71), 0)
    owners_keys = jax.random.split(jax.random.fold_in(keys[2], 1), N_LON * NLAT // LAT_DEV)
    owners_turns = jax.random.permutation(jax.random.fold_in(keys[2], 3), N_LON * NLAT // LAT_DEV)
    owners = jax.vmap(lambda own, number: routed_block(jax.random.fold_in(keys[2], 2), own, number, LAT_DEV, DEVICES, 1, CAP, 2))(owners_keys, owners_turns).reshape((N_LON, NLAT, 1))
    source_rows = plant(jax.random.randint(keys[3], (N_LON, NLAT), 0, LAT_DEV), jax.random.fold_in(keys[3], 1), 0, LAT_DEV - 1).astype(jnp.int32)
    cutoffs = draw_cutoffs(jax.random.fold_in(keys[6], 71), 0)
    stiffness = draw_stiffness(jax.random.fold_in(keys[6], 71), 0)
    return dict(state=state, weights=weights, owners=owners, source_rows=source_rows, cutoffs=cutoffs, stiffness=stiffness)


def lon_diff(field):
    return jnp.roll(field, -1, axis=2) - jnp.roll(field, 1, axis=2)


def lat_diff(field):
    padded = jnp.pad(field, ((1, 1), (0, 0), (0, 0)))
    return padded[2:] - padded[:-2]


def operate(field, stiffness):
    padded = jnp.pad(field, ((1, 1), (0, 0), (0, 0)))
    beside = padded[2:] + padded[:-2] + jnp.roll(field, -1, axis=2) + jnp.roll(field, 1, axis=2)
    return (4.0 + stiffness) * field - beside


def reference(state, weights, owners, source_rows, cutoffs, stiffness):
    owner = owners[:, :, 0]
    band = owner % N_LAT
    block = owner // N_LAT
    grid_row = band * LAT_DEV + source_rows
    layered = state.reshape(NLAT, 3, LEV, N_LON, LON_DEV)

    def one_block(column):
        source = layered[grid_row[column], :, :, block[column], :]
        start = (column * LON_DEV).astype(jnp.int32)
        piece = lax.dynamic_slice_in_dim(weights, start, LON_DEV, 2)
        return jnp.einsum("rcli,rij->rclj", source.astype(jnp.float32), piece.astype(jnp.float32))

    arrived = lax.map(one_block, jnp.arange(N_LON, dtype=jnp.int32))
    arrived = jnp.transpose(arrived, (1, 2, 3, 0, 4)).reshape(NLAT, 3, LEV, NLON)
    polar_rows = jnp.concatenate([arrived[:POLAR], arrived[NLAT - POLAR:]], axis=0)
    spectrum = jnp.fft.rfft(polar_rows, axis=-1)
    waves = jnp.arange(NLON // 2 + 1, dtype=jnp.int32)
    keep = waves[None, :] <= cutoffs[:, None]
    spectrum = jnp.where(keep[:, None, None, :], spectrum, 0.0)
    smooth = jnp.fft.irfft(spectrum, n=NLON, axis=-1).astype(arrived.dtype)
    filtered = jnp.concatenate([smooth[:POLAR], arrived[POLAR:NLAT - POLAR], smooth[POLAR:]], axis=0)
    u_field = filtered[:, 0]
    v_field = filtered[:, 1]
    theta = filtered[:, 2]
    rhs = theta - 0.5 * (lon_diff(u_field) + lat_diff(v_field))
    phi = jnp.zeros_like(rhs)
    residual = rhs
    direction = rhs
    norm_now = jnp.sum(residual * residual)
    for step in range(ITERS):
        image = operate(direction, stiffness)
        alpha = norm_now / jnp.sum(direction * image)
        phi = phi + alpha * direction
        residual = residual - alpha * image
        norm_next = jnp.sum(residual * residual)
        direction = residual + (norm_next / norm_now) * direction
        norm_now = norm_next
    return jnp.stack([u_field - 0.5 * lon_diff(phi), v_field - 0.5 * lat_diff(phi), theta - phi], axis=1)
```

```python
import numpy as np
import jax
import jax.numpy as jnp
from jax import lax
from jax.sharding import PartitionSpec as P

ITERS = 5
BOTH = ("lon", "lat")
HIGHEST = lax.Precision.HIGHEST


def neighbours(block, axis, dim, width, wrap):
    count = lax.axis_size(axis)
    forward = [(i, (i + 1) % count) for i in range(count if wrap else count - 1)]
    backward = [(target, source) for source, target in forward]
    size = block.shape[dim]
    low = lax.ppermute(lax.slice_in_dim(block, size - width, size, axis=dim), axis, forward)
    high = lax.ppermute(lax.slice_in_dim(block, 0, width, axis=dim), axis, backward)
    return jnp.concatenate([low, block, high], axis=dim)


def extend(block, width):
    return neighbours(neighbours(block, "lon", 2, width, True), "lat", 0, width, False)


def exchange(block, axes):
    return lax.all_to_all(block, axes, split_axis=0, concat_axis=0, tiled=True)


def fetch(state, owner, wanted):
    devices = lax.axis_size("lon") * lax.axis_size("lat")
    rows = owner.shape[0]
    same = owner[:, None] == owner[None, :]
    order = jnp.arange(rows, dtype=jnp.int32)
    slot = jnp.sum(same & (order[None, :] < order[:, None]), axis=1).astype(jnp.int32)
    named = owner[None, :] == jnp.arange(devices, dtype=jnp.int32)[:, None]
    requests = jnp.stack(
        [jnp.sum(jnp.where(named & (slot == s)[None, :], wanted[None, :], 0), axis=1) for s in range(2)],
        axis=1,
    )
    blocks = state[exchange(requests, BOTH)]
    moved = exchange(blocks, BOTH)
    return moved[owner, slot]


def low_pass(lines, cutoff):
    parts, count, points = lines.shape
    total = parts * points
    half = parts // 2 + 1
    d = np.arange(parts)
    k1 = np.arange(half)
    p = np.arange(points)
    first = 2 * np.pi * np.outer(k1, d) / parts
    twist = 2 * np.pi * np.outer(k1, p) / total
    inner = 2 * np.pi * np.outer(p, p) / points
    f32 = lambda a: jnp.asarray(a, jnp.float32)
    real = jnp.einsum("kd,dmp->kmp", f32(np.cos(first)), lines, precision=HIGHEST)
    imag = jnp.einsum("kd,dmp->kmp", f32(-np.sin(first)), lines, precision=HIGHEST)
    tc, ts = f32(np.cos(twist))[:, None, :], f32(np.sin(twist))[:, None, :]
    both = jnp.concatenate([real * tc + imag * ts, imag * tc - real * ts], axis=2)
    c, s = np.cos(inner), np.sin(inner)
    forward = f32(np.block([[c, -s], [s, c]]))
    inverse = f32(np.block([[c, s], [-s, c]]))
    spectrum = jnp.einsum("kmp,pq->kmq", both, forward, precision=HIGHEST)
    wave = jnp.asarray(k1[:, None] + parts * p[None, :], jnp.int32)
    kept = ((wave <= cutoff) | (wave >= total - cutoff)).astype(jnp.float32) / total
    kept = jnp.concatenate([kept, kept], axis=1)[:, None, :]
    back = jnp.einsum("kmp,pq->kmq", spectrum * kept, inverse, precision=HIGHEST)
    br, bi = back[..., :points], back[..., points:]
    weight = np.where((k1 == 0) | (k1 == parts // 2), 1.0, 2.0)[:, None]
    dr = br * tc - bi * ts
    di = br * ts + bi * tc
    return jnp.einsum("kd,kmp->dmp", f32(weight * np.cos(first)), dr, precision=HIGHEST) - jnp.einsum(
        "kd,kmp->dmp", f32(weight * np.sin(first)), di, precision=HIGHEST
    )


def solve(moments):
    squares, cross = moments[: ITERS], moments[ITERS :]
    mu = [squares[0], cross[0]]
    for k in range(1, ITERS):
        mu += [2.0 * squares[k] - mu[0], 2.0 * cross[k] - mu[1]]

    def inner(a, b):
        terms = [a[i] * b[j] * (0.5 * (mu[i + j] + mu[abs(i - j)])) for i in range(len(a)) for j in range(len(b))]
        return sum(terms)

    def image_of(a):
        out = [4.5 * x for x in a] + [0.0]
        for k, x in enumerate(a):
            out[k + 1] = out[k + 1] + 2.25 * x
            out[abs(k - 1)] = out[abs(k - 1)] + 2.25 * x
        return out

    phi = []
    residual = [jnp.float32(1.0)]
    direction = residual
    norm = mu[0]
    for step in range(ITERS):
        image = image_of(direction)
        alpha = norm / inner(direction, image)
        phi = [x + alpha * y for x, y in zip(phi + [0.0], direction)]
        if step < ITERS - 1:
            residual = [x - alpha * y for x, y in zip(residual + [0.0], image)]
            following = inner(residual, residual)
            ratio = following / norm
            direction = [x + ratio * y for x, y in zip(residual, direction + [0.0])]
            norm = following
    return phi


def shards(state, weights, owners, source_rows, cutoffs, stiffness):
    rows, _, levels, points = state.shape
    n_lon = lax.axis_size("lon")
    n_lat = lax.axis_size("lat")
    band = lax.axis_index("lat")
    north, south = band == 0, band == n_lat - 1
    depth = ITERS + 1
    stiff = extend(stiffness, depth)
    sources = fetch(state, owners[0, :, 0], source_rows[0]).reshape(rows, 3 * levels, points)
    arrived = jnp.einsum("bci,bij->bcj", sources, weights, preferred_element_type=jnp.float32)
    polar = cutoffs.shape[0] // 2
    start = jnp.where(north, 0, rows - polar).astype(jnp.int32)
    caps = lax.dynamic_slice_in_dim(arrived, start, polar, 0)
    lines = exchange(caps.reshape(n_lon, -1, points), "lon")
    line = lax.axis_index("lon") * polar // n_lon
    cutoff = cutoffs[jnp.where(north, line, polar + line)]
    smooth = exchange(low_pass(lines, cutoff), "lon").reshape(caps.shape)
    filtered = lax.dynamic_update_slice_in_dim(arrived, jnp.where(north | south, smooth, caps), start, 0)
    wide = extend(filtered, depth)
    u, v, theta = wide[:, :levels], wide[:, levels : 2 * levels], wide[:, 2 * levels :]
    place = jnp.arange(rows + 2 * depth) - depth + band * rows
    inside = ((place >= 0) & (place < n_lat * rows)).astype(jnp.float32)[:, None, None]

    def core(a, b):
        return a[1:-1, :, 1:-1], b

    def beside(p):
        return p[2:, :, 1:-1] + p[:-2, :, 1:-1] + p[1:-1, :, 2:] + p[1:-1, :, :-2]

    divergence = u[1:-1, :, 2:] - u[1:-1, :, :-2] + (v[2:, :, 1:-1] - v[:-2, :, 1:-1])
    table = [(theta[1:-1, :, 1:-1] - 0.5 * divergence) * inside[1:-1]]
    slope = (4.0 / 9.0) * (stiff - 0.5)
    squares, cross = [], []
    for k in range(ITERS):
        last = table[-1]
        w = depth - 2 - k
        cut = k + 2
        twice = slope[cut:-cut, :, cut:-cut] * last[1:-1, :, 1:-1] - (4.0 / 9.0) * beside(last)
        following = 0.5 * twice if k == 0 else twice - table[-2][2:-2, :, 2:-2]
        following = following * inside[cut:-cut]
        table.append(following)
    cores = []
    for k, t in enumerate(table):
        w = depth - 1 - k
        cores.append(t[w : w + rows, :, w : w + points])
    squares = [jnp.sum(cores[k] * cores[k]) for k in range(ITERS)]
    cross = [jnp.sum(cores[k] * cores[k + 1]) for k in range(ITERS)]
    moments = jnp.stack(squares + cross)
    spread = exchange(jnp.broadcast_to(moments[None], (n_lon * n_lat, 2 * ITERS)), BOTH)
    coefficients = solve(jnp.sum(spread, axis=0))
    phi = 0.0
    for k in range(ITERS):
        w = ITERS - 1 - k
        t = table[k]
        phi = phi + coefficients[k] * (t[w:-w, :, w:-w] if w else t)
    centre = filtered
    u_new = centre[:, :levels] - 0.5 * (phi[1:-1, :, 2:] - phi[1:-1, :, :-2])
    v_new = centre[:, levels : 2 * levels] - 0.5 * (phi[2:, :, 1:-1] - phi[:-2, :, 1:-1])
    t_new = centre[:, 2 * levels :] - phi[1:-1, :, 1:-1]
    return jnp.stack([u_new, v_new, t_new], axis=1)


def solution(mesh):
    in_specs = (
        P("lat", None, None, "lon"),
        P("lat", None, "lon"),
        P("lon", "lat", None),
        P("lon", "lat"),
        P(),
        P("lat", None, "lon"),
    )
    out_specs = P("lat", None, None, "lon")
    return jax.shard_map(shards, mesh=mesh, in_specs=in_specs, out_specs=out_specs, check_vma=False)
```

```python
import functools

import numpy as np
import jax
import jax.numpy as jnp
from jax import lax
from jax.experimental import pallas as pl
from jax.experimental.pallas import tpu as pltpu
from jax.sharding import PartitionSpec as P

ITERS = 5
BOTH = ("lon", "lat")
HIGHEST = lax.Precision.HIGHEST
FIELD = 16
FIELDS = 8
F32 = jnp.float32
MIB = 1024 * 1024


def params(mib):
    return pltpu.CompilerParams(vmem_limit_bytes=mib * MIB)


def in_hbm(x):
    return pltpu.with_memory_space_constraint(x, pltpu.HBM)


def exchange(block, axes):
    return lax.all_to_all(block, axes, split_axis=0, concat_axis=0, tiled=True)


def lanes(shape):
    return lax.broadcasted_iota(jnp.int32, shape, len(shape) - 1)


def pack_lanes(shape, rows):
    field = lanes(shape) // FIELD
    packed = jnp.zeros(shape, F32)
    for f, row in enumerate(rows):
        packed = jnp.where(field == f, pltpu.roll(row, (FIELD * f + 8) % 128, len(shape) - 1), packed)
    return packed


def unpack_lanes(packed, f):
    return pltpu.roll(packed, (-(FIELD * f + 8)) % 128, packed.ndim - 1)


def request_kernel(row_ref, wanted_ref, request_ref, place_ref):
    row = row_ref[...]
    size = row.shape[1]
    down = lax.broadcasted_iota(jnp.int32, (size, size), 0)
    across = lax.broadcasted_iota(jnp.int32, (size, size), 1)
    owner = jnp.broadcast_to(row, (size, size))
    earlier = (owner.T == owner) & (down < across)
    slot = jnp.sum(jnp.where(earlier, 1.0, 0.0), axis=0, keepdims=True)
    wanted = wanted_ref[...].astype(F32)
    out = jnp.zeros((size, size), F32)
    for s in range(2):
        hit = jnp.where((owner == down) & (slot == s), wanted, 0.0)
        out = jnp.where(across == s, jnp.sum(hit, axis=1, keepdims=True), out)
    request_ref[...] = out.astype(jnp.int32)
    place_ref[...] = 2 * row + slot.astype(jnp.int32)


def make_requests(owner, wanted):
    rows = wanted.shape[1]
    return pl.pallas_call(
        request_kernel,
        out_shape=(
            jax.ShapeDtypeStruct((rows, rows), jnp.int32),
            jax.ShapeDtypeStruct((1, rows), jnp.int32),
        ),
        cost_estimate=pl.CostEstimate(flops=200000, bytes_accessed=200000, transcendentals=0),
        compiler_params=params(2),
        name="requests",
    )(in_hbm(owner), in_hbm(wanted))


def ways(axis, wrap):
    count = lax.axis_size(axis)
    up = [(i, (i + 1) % count) for i in range(count if wrap else count - 1)]
    return up, [(b, a) for a, b in up]


def from_sides(to_east, to_west):
    east, west = ways("lon", True)
    return lax.ppermute(to_east, "lon", east), lax.ppermute(to_west, "lon", west)


def from_ends(last, first):
    north, south = ways("lat", False)
    return lax.ppermute(last, "lat", north), lax.ppermute(first, "lat", south)


def low_half(x):
    return lanes(x.shape) % FIELD < FIELD // 2


def shift(x, by):
    return pltpu.roll(x, by % 128, x.ndim - 1)


def for_sides(even, odd):
    low = low_half(even)
    return jnp.where(low, even, shift(odd, 8)), jnp.where(low, shift(even, -8), odd)


def merge(from_west, from_east, parity):
    low = low_half(from_west)
    if parity == 0:
        return jnp.where(low, from_west, shift(from_east, 8))
    return jnp.where(low, shift(from_west, -8), from_east)


def caps_kernel(place_ref, info_ref, moved_hbm, weights_hbm, caps_ref, held, weights_ref, sems, weights_sem):
    polar = caps_ref.shape[0]
    start = info_ref[0]
    copies = [
        pltpu.make_async_copy(moved_hbm.at[place_ref[start + i]], held.at[i], sems.at[i]) for i in range(polar)
    ]
    load = pltpu.make_async_copy(weights_hbm.at[pl.ds(start, polar)], weights_ref, weights_sem)
    load.start()
    for copy in copies:
        copy.start()
    load.wait()
    for copy in copies:
        copy.wait()
    rows = [jnp.dot(held[i], weights_ref[i], preferred_element_type=F32) for i in range(polar)]
    for i, row in enumerate(rows):
        caps_ref[i] = row


def make_caps(place, info, moved, weights, polar):
    _, depth, points = moved.shape
    smem = pl.BlockSpec(memory_space=pltpu.SMEM)
    hbm = pl.BlockSpec(memory_space=pl.ANY)
    return pl.pallas_call(
        caps_kernel,
        in_specs=[smem, smem, hbm, hbm],
        out_specs=pl.BlockSpec(memory_space=pltpu.VMEM),
        out_shape=jax.ShapeDtypeStruct((polar, depth, points), F32),
        scratch_shapes=[
            pltpu.VMEM((polar, depth, points), moved.dtype),
            pltpu.VMEM((polar, points, points), weights.dtype),
            pltpu.SemaphoreType.DMA((polar,)),
            pltpu.SemaphoreType.DMA,
        ],
        cost_estimate=pl.CostEstimate(flops=30000000, bytes_accessed=1200000, transcendentals=0),
        compiler_params=params(4),
        name="caps",
    )(place, info, in_hbm(moved), in_hbm(weights))


def arrive_kernel(
    place_ref, moved_hbm, stiffness_hbm, weights_hbm, arrived_hbm, east_ref, west_ref, ends_ref,
    moved_ref, stiffness_ref, weights_ref, arrived_ref, load_sems, weight_sems, save_sems,
):
    rows, depth, _ = arrived_ref.shape
    group = 2 * FIELDS
    pieces = rows // group
    loads = [
        pltpu.make_async_copy(moved_hbm, moved_ref, load_sems.at[0]),
        pltpu.make_async_copy(stiffness_hbm, stiffness_ref, load_sems.at[1]),
    ]

    def fetch(g):
        part = pl.ds(g * group, group)
        return pltpu.make_async_copy(weights_hbm.at[part], weights_ref.at[part], weight_sems.at[g])

    def save(g):
        part = pl.ds(g * group, group)
        return pltpu.make_async_copy(arrived_ref.at[part], arrived_hbm.at[part], save_sems.at[g])

    loads[0].start()
    fetch(0).start()
    loads[1].start()
    for g in range(1, pieces):
        fetch(g).start()
    for load in loads:
        load.wait()

    def pair(g, carry):
        fetch(g).wait()
        first = g * group
        sources = [moved_ref[place_ref[first + i]] for i in range(2 * FIELDS)]
        stiff = [stiffness_ref[first + i] for i in range(2 * FIELDS)]
        values = [
            jnp.dot(source, weights_ref[first + i], preferred_element_type=F32) for i, source in enumerate(sources)
        ]
        packed = [pack_lanes(values[0].shape, values[h * FIELDS : (h + 1) * FIELDS]) for h in range(2)]
        packed_stiff = [pack_lanes(stiff[0].shape, stiff[h * FIELDS : (h + 1) * FIELDS]) for h in range(2)]
        east, west = for_sides(*packed)
        east_stiff, west_stiff = for_sides(*packed_stiff)
        for i, value in enumerate(values):
            arrived_ref[first + i] = value
        east_ref[g, 0:depth] = east
        west_ref[g, 0:depth] = west
        east_ref[g, depth:] = east_stiff
        west_ref[g, depth:] = west_stiff
        save(g).start()
        return carry

    lax.fori_loop(0, rows // (2 * FIELDS), pair, 0)
    for f in range(FIELDS):
        for end, row in enumerate((f, rows - FIELDS + f)):
            ends_ref[end, f, 0:depth] = arrived_ref[row]
            ends_ref[end, f, depth:] = stiffness_ref[row]
    for g in range(pieces):
        save(g).wait()


def make_arrived(place, moved, weights, stiffness):
    _, depth, points = moved.shape
    rows, levels, _ = stiffness.shape
    both = depth + levels
    vmem = pl.BlockSpec(memory_space=pltpu.VMEM)
    hbm = pl.BlockSpec(memory_space=pl.ANY)
    side = jax.ShapeDtypeStruct((rows // (2 * FIELDS), both, points), F32)
    return pl.pallas_call(
        arrive_kernel,
        in_specs=[pl.BlockSpec(memory_space=pltpu.SMEM), hbm, hbm, hbm],
        out_specs=[hbm] + [vmem] * 3,
        out_shape=(
            pltpu.HBM((rows, depth, points), F32), side, side,
            jax.ShapeDtypeStruct((2, FIELDS, both, points), F32),
        ),
        scratch_shapes=[
            pltpu.VMEM(moved.shape, moved.dtype),
            pltpu.VMEM(stiffness.shape, F32),
            pltpu.VMEM(weights.shape, weights.dtype),
            pltpu.VMEM((rows, depth, points), F32),
            pltpu.SemaphoreType.DMA((2,)),
            pltpu.SemaphoreType.DMA((rows // (2 * FIELDS),)),
            pltpu.SemaphoreType.DMA((rows // (2 * FIELDS),)),
        ],
        cost_estimate=pl.CostEstimate(flops=20000000000, bytes_accessed=30000000, transcendentals=0),
        compiler_params=params(18),
        name="arrive",
    )(place, in_hbm(moved), in_hbm(stiffness), in_hbm(weights))


def ends_kernel(ends_ref, west_ref, east_ref, last_ref, first_ref):
    pairs = west_ref.shape[0]
    first_ref[0:FIELDS] = ends_ref[0]
    last_ref[0:FIELDS] = ends_ref[1]
    first_ref[FIELDS] = merge(west_ref[0], east_ref[0], 0)
    last_ref[FIELDS] = merge(west_ref[pairs - 1], east_ref[pairs - 1], 1)


def make_ends(ends, west, east):
    _, _, both, points = ends.shape
    shape = jax.ShapeDtypeStruct((FIELDS + 1, both, points), F32)
    return pl.pallas_call(
        ends_kernel,
        out_shape=(shape, shape),
        cost_estimate=pl.CostEstimate(flops=100000, bytes_accessed=2000000, transcendentals=0),
        compiler_params=params(4),
        name="ends",
    )(ends, west, east)


def filter_tables(parts, points):
    total = parts * points
    half = parts // 2 + 1
    k1, p = np.arange(half), np.arange(points)
    twist = 2 * np.pi * np.outer(k1, p) / total
    inner = 2 * np.pi * np.outer(p, p) / points
    c, s = np.cos(inner), np.sin(inner)
    forward = np.block([[c, -s], [s, c]]).astype(np.float32)
    inverse = np.block([[c, s], [-s, c]]).astype(np.float32)
    return np.concatenate([np.cos(twist), np.sin(twist)]).astype(np.float32), forward, inverse


def filter_kernel(
    info_ref, lines_ref, twist_hbm, forward_hbm, inverse_hbm, out_ref,
    work, back, twist_ref, forward_ref, inverse_ref, sems,
):
    parts, count, points = lines_ref.shape
    pairs = [(twist_hbm, twist_ref), (forward_hbm, forward_ref), (inverse_hbm, inverse_ref)]
    loads = [pltpu.make_async_copy(a, b, sems.at[i]) for i, (a, b) in enumerate(pairs)]
    for load in loads:
        load.start()
    total = parts * points
    mid = parts // 2
    cutoff = info_ref[4]
    tiles = count // 8
    loads[0].wait()
    c = [float(np.cos(2 * np.pi * i / parts)) for i in range(parts)]
    s = [float(np.sin(2 * np.pi * i / parts)) for i in range(parts)]
    for t in range(tiles):
        x = [lines_ref[d, 8 * t : 8 * t + 8, :] for d in range(parts)]
        even = [x[d] + x[parts - d] for d in range(1, mid)]
        odd = [x[d] - x[parts - d] for d in range(1, mid)]
        for k in range(mid + 1):
            real = x[0] + x[mid] if k % 2 == 0 else x[0] - x[mid]
            for d in range(1, mid):
                real = real + c[d * k % parts] * even[d - 1]
            row = k * count + 8 * t
            tc, ts = twist_ref[k : k + 1, :], twist_ref[mid + 1 + k : mid + 2 + k, :]
            if k in (0, mid):
                work[row : row + 8, 0:points] = real * tc
                work[row : row + 8, points:] = -real * ts
            else:
                imag = sum(s[d * k % parts] * odd[d - 1] for d in range(1, mid))
                work[row : row + 8, 0:points] = real * tc - imag * ts
                work[row : row + 8, points:] = -imag * tc - real * ts
    loads[1].wait()
    spectrum = jnp.dot(work[...], forward_ref[...], precision=HIGHEST, preferred_element_type=F32)
    shape = spectrum.shape
    wave = lax.broadcasted_iota(jnp.int32, shape, 0) // count + parts * (lanes(shape) % points)
    kept = (wave <= cutoff) | (wave >= total - cutoff)
    spectrum = jnp.where(kept, spectrum * (1.0 / total), 0.0)
    loads[2].wait()
    back[...] = jnp.dot(spectrum, inverse_ref[...], precision=HIGHEST, preferred_element_type=F32)
    for t in range(tiles):
        real, imag = [], []
        for k in range(mid + 1):
            row = k * count + 8 * t
            br, bi = back[row : row + 8, 0:points], back[row : row + 8, points:]
            tc, ts = twist_ref[k : k + 1, :], twist_ref[mid + 1 + k : mid + 2 + k, :]
            if k in (0, mid):
                real.append(br * tc - bi * ts)
                imag.append(None)
            else:
                real.append(2.0 * (br * tc - bi * ts))
                imag.append(2.0 * (br * ts + bi * tc))
        for d in range(mid + 1):
            even = real[0] + real[mid] if d % 2 == 0 else real[0] - real[mid]
            for k in range(1, mid):
                even = even + c[d * k % parts] * real[k]
            if d in (0, mid):
                out_ref[d, 8 * t : 8 * t + 8, :] = even
            else:
                odd = sum(s[d * k % parts] * imag[k] for k in range(1, mid))
                out_ref[d, 8 * t : 8 * t + 8, :] = even - odd
                out_ref[parts - d, 8 * t : 8 * t + 8, :] = even + odd
    shape = (8, points)
    low = lanes(shape) < points // 2
    for d in range(parts):
        rows = [
            jnp.where(
                low,
                out_ref[(d + 1) % parts, 8 * t : 8 * t + 8, :],
                out_ref[(d - 1) % parts, 8 * t : 8 * t + 8, :],
            )
            for t in range(tiles)
        ]
        out_ref[d, count : count + 8, :] = pack_lanes(shape, rows)


def low_pass(info, lines):
    parts, count, points = lines.shape
    tables = filter_tables(parts, points)
    rows = (parts // 2 + 1) * count
    vmem = pl.BlockSpec(memory_space=pltpu.VMEM)
    return pl.pallas_call(
        filter_kernel,
        in_specs=[pl.BlockSpec(memory_space=pltpu.SMEM)] + [vmem] + [pl.BlockSpec(memory_space=pl.ANY)] * 3,
        out_specs=vmem,
        out_shape=pltpu.HBM((parts, count + 8, points), F32),
        scratch_shapes=[pltpu.VMEM((rows, 2 * points), F32)] * 2
        + [pltpu.VMEM(x.shape, F32) for x in tables]
        + [pltpu.SemaphoreType.DMA((3,))],
        cost_estimate=pl.CostEstimate(flops=700000000, bytes_accessed=1400000, transcendentals=0),
        compiler_params=params(8),
        name="low_pass",
    )(info, lines, *[in_hbm(jnp.asarray(x)) for x in tables])


def split(x):
    high = x.astype(jnp.bfloat16)
    return high, (x - high.astype(F32)).astype(jnp.bfloat16)


def shift_matrix(rows, columns, left, right):
    source = lax.broadcasted_iota(jnp.int32, (rows, columns), 0)
    target = lax.broadcasted_iota(jnp.int32, (rows, columns), 1)
    west = (source + 1 == target) | ((source == rows - 1) & (target == 0))
    east = (source == target + 1) | ((source == 0) & (target == rows - 1))
    return (jnp.where(west, left, 0.0) + jnp.where(east, right, 0.0)).astype(jnp.bfloat16)


def shifted(x, matrix):
    flat = x.reshape(-1, x.shape[-1])
    high, low = split(flat)
    count = flat.shape[0]
    both = jnp.dot(jnp.concatenate([high, low], axis=0), matrix, preferred_element_type=F32)
    out = both[:count] + both[count:]
    return out.reshape(x.shape[:-1] + (matrix.shape[1],))


def basis_kernel(
    info_ref, arrived_hbm, west_hbm, east_hbm, above_hbm, below_hbm, stiffness_hbm, smooth_ref,
    filtered_hbm, t0, t1, t2, t3, t4, moments_ref,
    edge, filtered_ref, slope_ref, west_ref, east_ref, above_ref, below_ref, stiffness_ref, sems,
):
    rows, depth, points = filtered_ref.shape
    levels = depth // 3
    span = 2 * points
    groups = rows // FIELDS
    polar = smooth_ref.shape[0] // 2
    table = [t0, t1, t2, t3, t4]
    start, is_polar = info_ref[0], info_ref[1]
    top, bottom = info_ref[2].astype(F32), info_ref[3].astype(F32)
    stride = 32
    pairs = [
        (west_hbm, west_ref), (east_hbm, east_ref), (stiffness_hbm, stiffness_ref), (above_hbm, above_ref),
        (below_hbm, below_ref), (arrived_hbm, filtered_ref),
    ]
    loads = [pltpu.make_async_copy(a, b, sems.at[i]) for i, (a, b) in enumerate(pairs)]
    for load in loads:
        load.start()
    save = pltpu.make_async_copy(
        filtered_ref.at[pl.ds(start, polar)], filtered_hbm.at[pl.ds(start, polar)], sems.at[len(pairs)]
    )

    def unpack_group(first, packed, stiff):
        values = [unpack_lanes(packed, f) for f in range(FIELDS)]
        for f, value in enumerate(values):
            edge[first + f] = value[0:depth]
            slope_ref[first + f, :, 0:points] = (4.0 / 9.0) * (stiff[f] - 0.5)
            slope_ref[first + f, :, points:] = (4.0 / 9.0) * (value[depth:] - 0.5)

    def unpack(g, carry):
        for parity in range(2):
            first = (2 * g + parity) * FIELDS
            stiff = [stiffness_ref[first + f] for f in range(FIELDS)]
            unpack_group(first + FIELDS, merge(west_ref[g], east_ref[g], parity), stiff)
        return carry

    for load in loads[:3]:
        load.wait()
    lax.fori_loop(0, groups // 2, unpack, 0)
    for load in loads[3:5]:
        load.wait()
    unpack_group(0, above_ref[FIELDS], [above_ref[f, depth:] for f in range(FIELDS)])
    unpack_group(FIELDS + rows, below_ref[FIELDS], [below_ref[f, depth:] for f in range(FIELDS)])
    loads[5].wait()

    @pl.when(is_polar == 1)
    def _():
        half = depth // 2

        def put(i, carry):
            for h in range(2):
                line = smooth_ref[2 * i + h]
                filtered_ref[start + i, h * half : (h + 1) * half] = line[0:half]
                for t in range(half // 8):
                    low = h * half + 8 * t
                    edge[FIELDS + start + i, low : low + 8] = unpack_lanes(line[half:], t)
            return carry

        lax.fori_loop(0, polar, put, 0)
        save.start()

    difference = shift_matrix(span, span, -0.5, 0.5)
    neighbours = shift_matrix(span, span, 1.0, 1.0)

    def centre_of(e, count, part):
        low, high = part * levels, (part + 1) * levels
        rows_of = lambda ref, first: ref[pl.ds(first, count), low:high]
        if not isinstance(e, int) or FIELDS <= e < FIELDS + rows:
            centre = rows_of(filtered_ref, e - FIELDS)
        elif e < FIELDS:
            centre = rows_of(above_ref, e)
        else:
            centre = rows_of(below_ref, e - FIELDS - rows)
        return jnp.concatenate([centre, edge[pl.ds(e, count), low:high]], axis=2)

    def rhs(u, theta, north, south):
        return theta - (shifted(u, difference) + 0.5 * (south - north))

    def inner_rhs(e, count):
        return rhs(
            centre_of(e, count, 0), centre_of(e, count, 2), centre_of(e - 1, count, 1), centre_of(e + 1, count, 1)
        )

    def centre_rhs(i, carry):
        e = FIELDS + 1 + i * 14
        t0[pl.ds(e, 14)] = inner_rhs(e, 14)
        return carry

    lax.fori_loop(0, (rows - 2) // 14, centre_rhs, 0)
    first, last = FIELDS, FIELDS + rows - 1
    reach = ITERS
    t0[first - reach : first - 1] = top * inner_rhs(first - reach, reach - 1)
    t0[last + 2 : last + 1 + reach] = bottom * inner_rhs(last + 2, reach - 1)
    for e, scale in ((first - 1, top), (first, None), (last, None), (last + 1, bottom)):
        value = inner_rhs(e, 1)
        t0[e : e + 1] = value if scale is None else value * scale

    sums = []
    for k in range(ITERS):
        now = table[k]

        def following(e, count):
            here = now[pl.ds(e, count)]
            beside = shifted(here, neighbours) + (now[pl.ds(e - 1, count)] + now[pl.ds(e + 1, count)])
            twice = slope_ref[pl.ds(e, count)] * here - (4.0 / 9.0) * beside
            if k == 0:
                return here, 0.5 * twice
            return here, twice - table[k - 1][pl.ds(e, count)]

        def step(i, carry):
            squares, cross = carry
            e = FIELDS + i * stride
            here, value = following(e, stride)
            if k < ITERS - 1:
                table[k + 1][pl.ds(e, stride)] = value
            here, value = here[:, :, 0:points], value[:, :, 0:points]
            return squares + jnp.sum(here * here, axis=0), cross + jnp.sum(here * value, axis=0)

        zero = jnp.zeros((levels, points), F32)
        sums.append(lax.fori_loop(0, rows // stride, step, (zero, zero)))
        if k < ITERS - 1:
            reach = ITERS - 1 - k
            for e, scale in ((FIELDS - reach, top), (FIELDS + rows, bottom)):
                table[k + 1][e : e + reach] = scale * following(e, reach)[1]

    lane = lanes((1, points))
    moments = jnp.zeros((1, points), F32)
    for i, value in enumerate([a for a, _ in sums] + [b for _, b in sums]):
        total = jnp.sum(jnp.sum(value, axis=0, keepdims=True), axis=1, keepdims=True)
        moments = jnp.where(lane == i, total, moments)
    moments_ref[...] = jnp.broadcast_to(moments, moments_ref.shape)

    @pl.when(is_polar == 1)
    def _():
        save.wait()


def make_basis(info, arrived, west, east, above, below, stiffness, smooth, devices):
    rows, depth, points = arrived.shape
    levels = depth // 3
    extent = rows + 2 * FIELDS
    vmem = pl.BlockSpec(memory_space=pltpu.VMEM)
    hbm = pl.BlockSpec(memory_space=pl.ANY)
    halo = [west, east, above, below, stiffness]
    return pl.pallas_call(
        basis_kernel,
        in_specs=[pl.BlockSpec(memory_space=pltpu.SMEM)] + [hbm] * 6 + [vmem],
        out_specs=(hbm,) + (vmem,) * (ITERS + 1),
        out_shape=(pltpu.HBM((rows, depth, points), F32),)
        + (pltpu.VMEM((extent, levels, 2 * points), F32),) * ITERS
        + (jax.ShapeDtypeStruct((devices, points), F32),),
        scratch_shapes=[
            pltpu.VMEM((extent, depth, points), F32),
            pltpu.VMEM((rows, depth, points), F32),
            pltpu.VMEM((extent, levels, 2 * points), F32),
        ]
        + [pltpu.VMEM(x.shape, F32) for x in halo]
        + [pltpu.SemaphoreType.DMA((7,))],
        input_output_aliases={1: 0},
        cost_estimate=pl.CostEstimate(flops=40000000, bytes_accessed=24000000, transcendentals=0),
        compiler_params=params(24),
        name="basis",
    )(info, in_hbm(arrived), *[in_hbm(x) for x in halo], smooth)


def tree(terms):
    while len(terms) > 1:
        terms = [a + b for a, b in zip(terms[::2], terms[1::2])] + terms[len(terms) // 2 * 2 :]
    return terms[0]


def solve(mu):
    gram = [[0.5 * (mu[i + j] + mu[abs(i - j)]) for j in range(ITERS + 1)] for i in range(ITERS)]

    def inner(a, b):
        return tree([x * tree([y * gram[i][j] for j, y in enumerate(b)]) for i, x in enumerate(a)])

    def image_of(a):
        out = [4.5 * x for x in a] + [jnp.zeros_like(a[0])]
        for k, x in enumerate(a):
            out[k + 1] = out[k + 1] + 2.25 * x
            out[abs(k - 1)] = out[abs(k - 1)] + 2.25 * x
        return out

    zero = jnp.zeros_like(mu[0])
    phi = []
    residual = [zero + 1.0]
    direction = residual
    norm = mu[0]
    for step in range(ITERS):
        image = image_of(direction)
        alpha = norm / inner(direction, image)
        phi = [x + alpha * y for x, y in zip(phi + [zero], direction)]
        if step < ITERS - 1:
            residual = [x - alpha * y for x, y in zip(residual + [zero], image)]
            following = inner(residual, residual)
            ratio = following / norm
            direction = [x + ratio * y for x, y in zip(residual, direction + [zero])]
            norm = following
    return phi


def finish_kernel(spread_ref, filtered_hbm, t0, t1, t2, t3, t4, out_ref, coefficient_ref, filtered_ref, sems):
    table = [t0, t1, t2, t3, t4]
    _, levels, span = t0.shape
    points = span // 2
    block = out_ref.shape[0]
    g = pl.program_id(0)

    def fetch(i):
        part = pl.ds(i * block, block)
        return pltpu.make_async_copy(filtered_hbm.at[part], filtered_ref.at[part], sems.at[i])

    @pl.when(g == 0)
    def _():
        for i in range(filtered_ref.shape[0] // block):
            fetch(i).start()
        total = jnp.sum(spread_ref[...], axis=0, keepdims=True)
        lane = lanes(total.shape)
        picked = [
            jnp.sum(jnp.where(lane == i, total, 0.0), axis=1, keepdims=True) for i in range(2 * ITERS)
        ]
        mu = [picked[0], picked[ITERS]]
        for k in range(1, ITERS):
            mu += [2.0 * picked[k] - mu[0], 2.0 * picked[ITERS + k] - mu[1]]
        for k, value in enumerate(solve(mu)):
            coefficient_ref[k] = jnp.broadcast_to(value, (8, points))

    c = [
        jnp.concatenate([jnp.concatenate([coefficient_ref[k]] * (levels // 8), axis=0)] * 2, axis=1)
        for k in range(ITERS)
    ]

    fetch(g).wait()

    def phi_of(e):
        return tree([c[k] * table[k][e] for k in range(ITERS)])

    stride = 4

    def step(i, carry):
        before, here = carry
        first = i * stride
        e = FIELDS + g * block + first
        near = [before, here] + [phi_of(e + 1 + j) for j in range(stride)]
        old = [filtered_ref[g * block + first + j] for j in range(stride)]
        new = []
        for j in range(stride):
            here = near[j + 1]
            across = pltpu.roll(here, span - 1, 1) - pltpu.roll(here, 1, 1)
            new.append(old[j][0:levels] - 0.5 * across[:, 0:points])
            new.append(old[j][levels : 2 * levels] - 0.5 * (near[j + 2] - near[j])[:, 0:points])
            new.append(old[j][2 * levels :] - here[:, 0:points])
        for j in range(stride):
            for part in range(3):
                out_ref[first + j, part * levels : (part + 1) * levels] = new[3 * j + part]
        return near[stride], near[stride + 1]

    e = FIELDS + g * block
    lax.fori_loop(0, block // stride, step, (phi_of(e - 1), phi_of(e)))


def finish(spread, filtered, table):
    rows, depth, points = filtered.shape
    block = 32
    vmem = pl.BlockSpec(memory_space=pltpu.VMEM)
    piece = pl.BlockSpec((block, depth, points), lambda g: (g, 0, 0))
    return pl.pallas_call(
        finish_kernel,
        grid=(rows // block,),
        in_specs=[vmem, pl.BlockSpec(memory_space=pl.ANY)] + [vmem] * ITERS,
        out_specs=piece,
        out_shape=jax.ShapeDtypeStruct((rows, depth, points), F32),
        scratch_shapes=[
            pltpu.VMEM((ITERS, 8, points), F32),
            pltpu.VMEM((rows, depth, points), F32),
            pltpu.SemaphoreType.DMA((rows // block,)),
        ],
        cost_estimate=pl.CostEstimate(flops=20000000, bytes_accessed=17000000, transcendentals=0),
        compiler_params=params(12),
        name="finish",
    )(spread, in_hbm(filtered), *table)


def shards(state, weights, owners, source_rows, cutoffs, stiffness):
    rows, comps, levels, points = state.shape
    depth = comps * levels
    n_lon = lax.axis_size("lon")
    n_lat = lax.axis_size("lat")
    devices = n_lon * n_lat
    band = lax.axis_index("lat")
    north, south = band == 0, band == n_lat - 1
    polar = cutoffs.shape[0] // 2
    line = lax.axis_index("lon") * polar // n_lon
    info = jnp.stack(
        [
            jnp.where(north, 0, rows - polar),
            (north | south).astype(jnp.int32),
            (band > 0).astype(jnp.int32),
            (band < n_lat - 1).astype(jnp.int32),
            cutoffs[jnp.where(north, line, polar + line)],
        ]
    ).astype(jnp.int32)

    requests, place = make_requests(owners[:, :, 0], source_rows)
    asked = exchange(requests, BOTH)[:, :2]
    moved = exchange(state[asked], BOTH).reshape(2 * devices, depth, points)

    place = place[0]
    caps = make_caps(place, info, moved, weights, polar)
    lines = exchange(caps.reshape(n_lon, -1, points), "lon")
    place, caps = lax.optimization_barrier((place, caps))
    arrived, to_east, to_west, ends = make_arrived(place, moved, weights, stiffness)
    west, east = from_sides(to_east, to_west)
    smooth = exchange(low_pass(info, lines), "lon")
    above, below = from_ends(*make_ends(ends, west, east))
    filtered, *table, moments = make_basis(
        info, arrived, west, east, above, below, stiffness, smooth, devices
    )
    out = finish(exchange(moments, BOTH), filtered, table)
    return out.reshape(rows, comps, levels, points)


def solution(mesh):
    in_specs = (
        P("lat", None, None, "lon"),
        P("lat", None, "lon"),
        P("lon", "lat", None),
        P("lon", "lat"),
        P(),
        P("lat", None, "lon"),
    )
    out_specs = P("lat", None, None, "lon")
    return jax.shard_map(shards, mesh=mesh, in_specs=in_specs, out_specs=out_specs, check_vma=False)
```

```python
import functools

import numpy as np
import jax
import jax.numpy as jnp
from jax import lax
from jax.experimental import pallas as pl
from jax.experimental.pallas import tpu as pltpu
from jax.sharding import PartitionSpec as P

ITERS = 5
BOTH = ("lon", "lat")
HIGHEST = lax.Precision.HIGHEST
FIELD = 16
FIELDS = 8
F32 = jnp.float32
MIB = 1024 * 1024


def params(mib):
    return pltpu.CompilerParams(vmem_limit_bytes=mib * MIB)


def in_hbm(x):
    return pltpu.with_memory_space_constraint(x, pltpu.HBM)


def exchange(block, axes):
    return lax.all_to_all(block, axes, split_axis=0, concat_axis=0, tiled=True)


def lanes(shape):
    return lax.broadcasted_iota(jnp.int32, shape, len(shape) - 1)


def pack_lanes(shape, rows):
    field = lanes(shape) // FIELD
    packed = jnp.zeros(shape, F32)
    for f, row in enumerate(rows):
        packed = jnp.where(field == f, pltpu.roll(row, (FIELD * f + 8) % 128, len(shape) - 1), packed)
    return packed


def unpack_lanes(packed, f):
    return pltpu.roll(packed, (-(FIELD * f + 8)) % 128, packed.ndim - 1)


def request_kernel(row_ref, wanted_ref, request_ref, place_ref):
    row = row_ref[...]
    size = row.shape[1]
    down = lax.broadcasted_iota(jnp.int32, (size, size), 0)
    across = lax.broadcasted_iota(jnp.int32, (size, size), 1)
    owner = jnp.broadcast_to(row, (size, size))
    earlier = (owner.T == owner) & (down < across)
    slot = jnp.sum(jnp.where(earlier, 1.0, 0.0), axis=0, keepdims=True)
    wanted = wanted_ref[...].astype(F32)
    out = jnp.zeros((size, size), F32)
    for s in range(2):
        hit = jnp.where((owner == down) & (slot == s), wanted, 0.0)
        out = jnp.where(across == s, jnp.sum(hit, axis=1, keepdims=True), out)
    request_ref[...] = out.astype(jnp.int32)
    place_ref[...] = 2 * row + slot.astype(jnp.int32)


def make_requests(owner, wanted):
    rows = wanted.shape[1]
    return pl.pallas_call(
        request_kernel,
        out_shape=(
            jax.ShapeDtypeStruct((rows, rows), jnp.int32),
            jax.ShapeDtypeStruct((1, rows), jnp.int32),
        ),
        cost_estimate=pl.CostEstimate(flops=200000, bytes_accessed=200000, transcendentals=0),
        compiler_params=params(2),
        name="requests",
    )(in_hbm(owner), in_hbm(wanted))


def ways(axis, wrap):
    count = lax.axis_size(axis)
    up = [(i, (i + 1) % count) for i in range(count if wrap else count - 1)]
    return up, [(b, a) for a, b in up]


def from_sides(to_east, to_west):
    east, west = ways("lon", True)
    return lax.ppermute(to_east, "lon", east), lax.ppermute(to_west, "lon", west)


def from_ends(last, first):
    north, south = ways("lat", False)
    return lax.ppermute(last, "lat", north), lax.ppermute(first, "lat", south)


def low_half(x):
    return lanes(x.shape) % FIELD < FIELD // 2


def shift(x, by):
    return pltpu.roll(x, by % 128, x.ndim - 1)


def for_sides(even, odd):
    low = low_half(even)
    return jnp.where(low, even, shift(odd, 8)), jnp.where(low, shift(even, -8), odd)


def strips(from_west, from_east, own, parity):
    low = low_half(own)
    if parity == 0:
        return jnp.where(low, from_west, own), jnp.where(low, own, shift(from_east, 8))
    return jnp.where(low, shift(from_west, -8), own), jnp.where(low, own, from_east)


def beyond(left, right):
    return jnp.where(lanes(left.shape) % FIELD == FIELD // 2, shift(left, 1), shift(right, -1))


def insertion(packed, f):
    lane = lanes(packed.shape)
    return jnp.where((lane == 0) | (lane == 127), unpack_lanes(packed, f), 0.0)


def insertions(packed, first, count):
    return jnp.stack([insertion(packed[(first + i) // FIELDS], (first + i) % FIELDS) for i in range(count)])


def caps_kernel(
    place_ref, info_ref, moved_hbm, weights_hbm, stiffness_hbm, caps_ref, last_ref, first_ref,
    held, weights_ref, stiffness_ref, row_sems, sems,
):
    polar = caps_ref.shape[0]
    depth = caps_ref.shape[1]
    rows = weights_hbm.shape[0]
    start = info_ref[0]
    spans = [(start, 0, polar), (0, polar, FIELDS), (rows - FIELDS, polar + FIELDS, FIELDS)]
    copies = []
    for n, (row, at, count) in enumerate(spans):
        copies.append(
            pltpu.make_async_copy(weights_hbm.at[pl.ds(row, count)], weights_ref.at[pl.ds(at, count)], sems.at[n])
        )
        copies += [
            pltpu.make_async_copy(moved_hbm.at[place_ref[row + i]], held.at[at + i], row_sems.at[at + i])
            for i in range(count)
        ]
    for end, row in enumerate((0, rows - FIELDS)):
        copies.append(
            pltpu.make_async_copy(stiffness_hbm.at[pl.ds(row, FIELDS)], stiffness_ref.at[end], sems.at[3 + end])
        )
    for copy in copies:
        copy.start()
    for copy in copies:
        copy.wait()
    values = [
        jnp.dot(held[i], weights_ref[i], preferred_element_type=F32) for i in range(polar + 2 * FIELDS)
    ]
    for i in range(polar):
        caps_ref[i] = values[i]
    for end, ref in enumerate((first_ref, last_ref)):
        low = polar + end * FIELDS
        rim = values[low : low + FIELDS]
        stiff = [stiffness_ref[end, f] for f in range(FIELDS)]
        for f in range(FIELDS):
            ref[f, 0:depth] = rim[f]
            ref[f, depth:] = stiff[f]
        ref[FIELDS, 0:depth] = pack_lanes(rim[0].shape, rim)
        ref[FIELDS, depth:] = pack_lanes(stiff[0].shape, stiff)


def make_caps(place, info, moved, weights, stiffness, polar):
    _, depth, points = moved.shape
    levels = stiffness.shape[1]
    smem = pl.BlockSpec(memory_space=pltpu.SMEM)
    hbm = pl.BlockSpec(memory_space=pl.ANY)
    count = polar + 2 * FIELDS
    rim = jax.ShapeDtypeStruct((FIELDS + 1, depth + levels, points), F32)
    return pl.pallas_call(
        caps_kernel,
        in_specs=[smem, smem, hbm, hbm, hbm],
        out_specs=[pl.BlockSpec(memory_space=pltpu.VMEM)] * 3,
        out_shape=(jax.ShapeDtypeStruct((polar, depth, points), F32), rim, rim),
        scratch_shapes=[
            pltpu.VMEM((count, depth, points), moved.dtype),
            pltpu.VMEM((count, points, points), weights.dtype),
            pltpu.VMEM((2, FIELDS, levels, points), F32),
            pltpu.SemaphoreType.DMA((count,)),
            pltpu.SemaphoreType.DMA((5,)),
        ],
        cost_estimate=pl.CostEstimate(flops=60000000, bytes_accessed=2400000, transcendentals=0),
        compiler_params=params(6),
        name="caps",
    )(place, info, in_hbm(moved), in_hbm(weights), in_hbm(stiffness))


def stiff_kernel(stiffness_ref, east_ref, west_ref, own_ref):
    def pair(g, carry):
        packed = []
        for h in range(2):
            rows = [stiffness_ref[(2 * g + h) * FIELDS + f] for f in range(FIELDS)]
            packed.append(pack_lanes(rows[0].shape, rows))
        east_ref[g], west_ref[g] = for_sides(*packed)
        own_ref[2 * g], own_ref[2 * g + 1] = packed
        return carry

    lax.fori_loop(0, east_ref.shape[0], pair, 0)


def pack_stiffness(stiffness):
    rows, levels, points = stiffness.shape
    side = pltpu.HBM((rows // (2 * FIELDS), levels, points), F32)
    return pl.pallas_call(
        stiff_kernel,
        out_shape=(side, side, pltpu.HBM((rows // FIELDS, levels, points), F32)),
        cost_estimate=pl.CostEstimate(flops=1000000, bytes_accessed=1300000, transcendentals=0),
        compiler_params=params(4),
        name="pack_stiffness",
    )(in_hbm(stiffness))


def edge_weights_kernel(weights_ref, out_ref):
    rows = [weights_ref[f].astype(F32) for f in range(FIELDS)]
    out_ref[0] = pack_lanes(rows[0].shape, rows).astype(out_ref.dtype)


def edge_weights(weights):
    rows, points, _ = weights.shape
    return pl.pallas_call(
        edge_weights_kernel,
        grid=(rows // FIELDS,),
        in_specs=[pl.BlockSpec((FIELDS, points, points), lambda g: (g, 0, 0))],
        out_specs=pl.BlockSpec((1, points, points), lambda g: (g, 0, 0)),
        out_shape=pltpu.HBM((rows // FIELDS, points, points), weights.dtype),
        cost_estimate=pl.CostEstimate(flops=2000000, bytes_accessed=5000000, transcendentals=0),
        compiler_params=params(6),
        name="edge_weights",
    )(in_hbm(weights))


def edges_kernel(
    place_ref, moved_hbm, east_hbm, west_hbm, own_hbm, weights_hbm, east_ref, west_ref, own_ref,
    moved_ref, weights_ref, sems,
):
    depth = moved_ref.shape[1]
    levels = own_hbm.shape[1]
    loads = [
        pltpu.make_async_copy(moved_hbm, moved_ref, sems.at[0]),
        pltpu.make_async_copy(weights_hbm, weights_ref, sems.at[1]),
        pltpu.make_async_copy(east_hbm, east_ref.at[:, pl.ds(depth, levels)], sems.at[2]),
        pltpu.make_async_copy(west_hbm, west_ref.at[:, pl.ds(depth, levels)], sems.at[3]),
        pltpu.make_async_copy(own_hbm, own_ref.at[:, pl.ds(depth, levels)], sems.at[4]),
    ]
    for load in loads:
        load.start()
    for load in loads[:2]:
        load.wait()
    shape = (depth, moved_ref.shape[2])
    field = lanes(shape) // FIELD

    def pair(g, carry):
        packed = []
        for h in range(2):
            group = 2 * g + h
            sources = [moved_ref[place_ref[group * FIELDS + f]] for f in range(FIELDS)]
            product = jnp.dot(
                jnp.concatenate(sources, axis=0), weights_ref[group], preferred_element_type=F32
            )
            value = jnp.zeros(shape, F32)
            for f in range(FIELDS):
                value = jnp.where(field == f, product[f * depth : (f + 1) * depth], value)
            packed.append(value)
        east, west = for_sides(*packed)
        east_ref[g, 0:depth] = east
        west_ref[g, 0:depth] = west
        for h in range(2):
            own_ref[2 * g + h, 0:depth] = packed[h]
        return carry

    lax.fori_loop(0, east_ref.shape[0], pair, 0, unroll=2)
    for load in loads[2:]:
        load.wait()


def make_edges(place, moved, weights, stiff):
    _, depth, points = moved.shape
    groups, levels, _ = stiff[2].shape
    both = depth + levels
    vmem = pl.BlockSpec(memory_space=pltpu.VMEM)
    hbm = pl.BlockSpec(memory_space=pl.ANY)
    side = jax.ShapeDtypeStruct((groups // 2, both, points), F32)
    return pl.pallas_call(
        edges_kernel,
        in_specs=[pl.BlockSpec(memory_space=pltpu.SMEM)] + [hbm] * 5,
        out_specs=[vmem] * 3,
        out_shape=(side, side, pltpu.HBM((groups, both, points), F32)),
        scratch_shapes=[
            pltpu.VMEM(moved.shape, moved.dtype),
            pltpu.VMEM(weights.shape, weights.dtype),
            pltpu.SemaphoreType.DMA((5,)),
        ],
        cost_estimate=pl.CostEstimate(flops=10000000000, bytes_accessed=5000000, transcendentals=0),
        compiler_params=params(10),
        name="edges",
    )(place, in_hbm(moved), *[in_hbm(x) for x in stiff], in_hbm(weights))


def ends_kernel(last_rim_ref, first_rim_ref, west_ref, east_ref, last_ref, first_ref):
    pairs = west_ref.shape[0]
    for rim, ref, end, pair in ((first_rim_ref, first_ref, 0, 0), (last_rim_ref, last_ref, 1, pairs - 1)):
        ref[0:FIELDS] = rim[0:FIELDS]
        ref[FIELDS], ref[FIELDS + 1] = strips(west_ref[pair], east_ref[pair], rim[FIELDS], end)


def make_ends(last, first, west, east):
    _, both, points = last.shape
    shape = jax.ShapeDtypeStruct((FIELDS + 2, both, points), F32)
    return pl.pallas_call(
        ends_kernel,
        out_shape=(shape, shape),
        cost_estimate=pl.CostEstimate(flops=100000, bytes_accessed=2000000, transcendentals=0),
        compiler_params=params(6),
        name="ends",
    )(last, first, west, east)


def tree(terms):
    while len(terms) > 1:
        terms = [a + b for a, b in zip(terms[::2], terms[1::2])] + terms[len(terms) // 2 * 2 :]
    return terms[0]


def halves(table):
    high = table.astype(jnp.bfloat16)
    return np.stack([high, (table - high.astype(np.float64)).astype(jnp.bfloat16)])


def filter_tables(parts, points):
    total = parts * points
    half = parts // 2 + 1
    k1, p = np.arange(half), np.arange(points)
    twist = 2 * np.pi * np.outer(k1, p) / total
    inner = 2 * np.pi * np.outer(p, p) / points
    c, s = np.cos(inner), np.sin(inner)
    forward = np.block([[c, -s], [s, c]])
    inverse = np.block([[c, s], [-s, c]])
    twist = np.concatenate([np.cos(twist), np.sin(twist)]).astype(np.float32)
    return twist, halves(forward), halves(inverse)


def cosine_sums(v, parts):
    mid, quarter = parts // 2, parts // 4
    plus = [v[j - 1] + v[mid - j - 1] for j in range(1, quarter)]
    minus = [v[j - 1] - v[mid - j - 1] for j in range(1, quarter)]
    out = []
    for m in range(mid + 1):
        folded = plus if m % 2 == 0 else minus
        terms = [float(np.cos(2 * np.pi * m * j / parts)) * folded[j - 1] for j in range(1, quarter)]
        if m % 2 == 0:
            terms.append(v[quarter - 1] if m % 4 == 0 else -v[quarter - 1])
        out.append(tree(terms))
    return out


def sine_sums(v, parts):
    mid, quarter = parts // 2, parts // 4
    plus = [v[j - 1] + v[mid - j - 1] for j in range(1, quarter)]
    minus = [v[j - 1] - v[mid - j - 1] for j in range(1, quarter)]
    out = []
    for m in range(1, mid):
        folded = minus if m % 2 == 0 else plus
        terms = [float(np.sin(2 * np.pi * m * j / parts)) * folded[j - 1] for j in range(1, quarter)]
        if m % 2 == 1:
            terms.append(v[quarter - 1] if m % 4 == 1 else -v[quarter - 1])
        out.append(tree(terms))
    return out


def product(x, table_ref):
    high, low = split(x)
    count = x.shape[0]
    both = jnp.dot(jnp.concatenate([high, low], axis=0), table_ref[0], preferred_element_type=F32)
    return both[:count] + both[count:] + jnp.dot(high, table_ref[1], preferred_element_type=F32)


def filter_kernel(
    info_ref, lines_ref, twist_hbm, forward_hbm, inverse_hbm, out_ref,
    work, back, twist_ref, forward_ref, inverse_ref, sems,
):
    parts, count, points = lines_ref.shape
    pairs = [(twist_hbm, twist_ref), (forward_hbm, forward_ref), (inverse_hbm, inverse_ref)]
    loads = [pltpu.make_async_copy(a, b, sems.at[i]) for i, (a, b) in enumerate(pairs)]
    for load in loads:
        load.start()
    total = parts * points
    mid = parts // 2
    cutoff = info_ref[4]
    tiles = count // 8
    loads[0].wait()
    for t in range(tiles):
        x = [lines_ref[d, 8 * t : 8 * t + 8, :] for d in range(parts)]
        even = cosine_sums([x[d] + x[parts - d] for d in range(1, mid)], parts)
        odd = sine_sums([x[d] - x[parts - d] for d in range(1, mid)], parts)
        ends = (x[0] + x[mid], x[0] - x[mid])
        for k in range(mid + 1):
            real = ends[k % 2] + even[k]
            row = k * count + 8 * t
            tc, ts = twist_ref[k : k + 1, :], twist_ref[mid + 1 + k : mid + 2 + k, :]
            if k in (0, mid):
                work[row : row + 8, 0:points] = real * tc
                work[row : row + 8, points:] = -real * ts
            else:
                imag = odd[k - 1]
                work[row : row + 8, 0:points] = real * tc - imag * ts
                work[row : row + 8, points:] = -imag * tc - real * ts
    loads[1].wait()
    spectrum = product(work[...], forward_ref)
    shape = spectrum.shape
    wave = lax.broadcasted_iota(jnp.int32, shape, 0) // count + parts * (lanes(shape) % points)
    kept = (wave <= cutoff) | (wave >= total - cutoff)
    spectrum = jnp.where(kept, spectrum * (1.0 / total), 0.0)
    loads[2].wait()
    back[...] = product(spectrum, inverse_ref)
    for t in range(tiles):
        real, imag = [], []
        for k in range(mid + 1):
            row = k * count + 8 * t
            br, bi = back[row : row + 8, 0:points], back[row : row + 8, points:]
            tc, ts = twist_ref[k : k + 1, :], twist_ref[mid + 1 + k : mid + 2 + k, :]
            real.append(br * tc - bi * ts)
            if k not in (0, mid):
                imag.append(br * ts + bi * tc)
        even = cosine_sums(real[1:mid], parts)
        odd = sine_sums(imag, parts)
        ends = (real[0] + real[mid], real[0] - real[mid])
        for d in range(mid + 1):
            value = ends[d % 2] + 2.0 * even[d]
            if d in (0, mid):
                out_ref[d, 8 * t : 8 * t + 8, :] = value
            else:
                out_ref[d, 8 * t : 8 * t + 8, :] = value - 2.0 * odd[d - 1]
                out_ref[parts - d, 8 * t : 8 * t + 8, :] = value + 2.0 * odd[d - 1]
    shape = (8, points)
    low = lanes(shape) < points // 2
    for d in range(parts):
        rows = [
            jnp.where(
                low,
                out_ref[(d + 1) % parts, 8 * t : 8 * t + 8, :],
                out_ref[(d - 1) % parts, 8 * t : 8 * t + 8, :],
            )
            for t in range(tiles)
        ]
        out_ref[d, count : count + 8, :] = pack_lanes(shape, rows)


def low_pass(info, lines):
    parts, count, points = lines.shape
    tables = filter_tables(parts, points)
    rows = (parts // 2 + 1) * count
    vmem = pl.BlockSpec(memory_space=pltpu.VMEM)
    return pl.pallas_call(
        filter_kernel,
        in_specs=[pl.BlockSpec(memory_space=pltpu.SMEM)] + [vmem] + [pl.BlockSpec(memory_space=pl.ANY)] * 3,
        out_specs=vmem,
        out_shape=pltpu.HBM((parts, count + 8, points), F32),
        scratch_shapes=[pltpu.VMEM((rows, 2 * points), F32)] * 2
        + [pltpu.VMEM(x.shape, x.dtype) for x in tables]
        + [pltpu.SemaphoreType.DMA((3,))],
        cost_estimate=pl.CostEstimate(flops=700000000, bytes_accessed=1400000, transcendentals=0),
        compiler_params=params(8),
        name="low_pass",
    )(info, lines, *[in_hbm(jnp.asarray(x)) for x in tables])


def split(x):
    high = x.astype(jnp.bfloat16)
    return high, (x - high.astype(F32)).astype(jnp.bfloat16)


def shift_matrix(points, left, right):
    source = lax.broadcasted_iota(jnp.int32, (2 * points, points), 0) % points
    target = lax.broadcasted_iota(jnp.int32, (2 * points, points), 1)
    west, east = source + 1 == target, source == target + 1
    return (jnp.where(west, left, 0.0) + jnp.where(east, right, 0.0)).astype(jnp.bfloat16)


def shifted(x, matrix):
    flat = x.reshape(-1, x.shape[-1])
    out = jnp.dot(jnp.concatenate(split(flat), axis=1), matrix, preferred_element_type=F32)
    return out.reshape(x.shape)


def prepare_kernel(
    place_ref, info_ref, moved_hbm, weights_hbm, west_hbm, east_hbm, own_hbm,
    arrived_hbm, begun_hbm, strips_ref, ends_ref,
    moved_ref, weights_ref, begun_ref, wide, past, west_ref, east_ref, own_ref, sems, weight_sems, row_sems, save_sems,
):
    rows, levels, points = begun_ref.shape
    depth = wide.shape[1]
    polar = 16
    pieces, stride = rows // polar, 2 * polar
    start, is_polar = info_ref[0], info_ref[1]
    pairs = [(west_hbm, west_ref), (east_hbm, east_ref), (own_hbm, own_ref), (moved_hbm, moved_ref)]
    loads = [pltpu.make_async_copy(a, b, sems.at[i]) for i, (a, b) in enumerate(pairs)]

    def fetch(i):
        piece = pl.ds(i * polar, polar)
        return pltpu.make_async_copy(weights_hbm.at[piece], weights_ref.at[piece], weight_sems.at[i])

    def save_rows(i):
        return pltpu.make_async_copy(
            wide.at[pl.ds(1 + i * polar, polar)], arrived_hbm.at[pl.ds(i * polar, polar)], row_sems.at[i]
        )

    def save(i):
        piece = pl.ds(i * stride, stride)
        return pltpu.make_async_copy(begun_ref.at[piece], begun_hbm.at[piece], save_sems.at[i])

    for load in loads:
        load.start()
    for i in range(pieces):
        fetch(i).start()
    zero = jnp.zeros((1, depth, points), F32)
    for row in (0, rows + 1):
        wide[row : row + 1] = zero
    for load in loads[:3]:
        load.wait()
    for g in range(rows // FIELDS):
        left, right = strips(west_ref[g // 2], east_ref[g // 2], own_ref[g], g % 2)
        strips_ref[0, g], strips_ref[1, g] = left, right
        past[g] = beyond(left[0:levels], right[0:levels])

    @pl.when(is_polar == 1)
    def _():
        past[pl.ds(start // FIELDS, polar // FIELDS)] = jnp.zeros((polar // FIELDS, levels, points), F32)

    loads[3].wait()
    difference = shift_matrix(points, -0.5, 0.5)
    half_sign = jnp.where(lanes((1, 1, points)) == 0, 0.5, -0.5)

    def interpolate(i):
        fetch(i).wait()
        first = i * polar
        sources = [moved_ref[place_ref[first + j]] for j in range(polar)]
        values = [
            jnp.dot(source, weights_ref[first + j], preferred_element_type=F32) for j, source in enumerate(sources)
        ]
        for j, value in enumerate(values):
            wide[1 + first + j] = value

        @pl.when((is_polar == 1) & (start // polar == i))
        def _():
            wide[1 + first : 1 + first + polar] = jnp.zeros((polar, depth, points), F32)

        save_rows(i).start()

    def step(i):
        e = 1 + i * stride
        part = lambda e, which: wide[pl.ds(e, stride), which * levels : (which + 1) * levels]
        groups = past[pl.ds(i * (stride // FIELDS), stride // FIELDS)]
        across = shifted(part(e, 0), difference) - half_sign * insertions(groups, 0, stride)
        begun_ref[pl.ds(i * stride, stride)] = part(e, 2) - (across + 0.5 * (part(e + 1, 1) - part(e - 1, 1)))
        save(i).start()

    for i in range(pieces):
        interpolate(i)
        if i % 2 == 0 and i > 0:
            step(i // 2 - 1)
    step(pieces // 2 - 1)
    ends_ref[0] = wide[1, levels : 2 * levels]
    ends_ref[1] = wide[rows, levels : 2 * levels]
    for i in range(pieces):
        save_rows(i).wait()
    for i in range(rows // stride):
        save(i).wait()


def prepare(place, info, moved, weights, west, east, own):
    rows, points, _ = weights.shape
    groups, both, _ = own.shape
    depth = moved.shape[1]
    levels = both - depth
    vmem = pl.BlockSpec(memory_space=pltpu.VMEM)
    hbm = pl.BlockSpec(memory_space=pl.ANY)
    return pl.pallas_call(
        prepare_kernel,
        in_specs=[pl.BlockSpec(memory_space=pltpu.SMEM)] * 2 + [hbm] * 5,
        out_specs=[hbm, hbm, vmem, vmem],
        out_shape=(
            pltpu.HBM((rows, depth, points), F32),
            pltpu.HBM((rows, levels, points), F32),
            pltpu.HBM((2, groups, both, points), F32),
            jax.ShapeDtypeStruct((2, levels, points), F32),
        ),
        scratch_shapes=[
            pltpu.VMEM(moved.shape, moved.dtype),
            pltpu.VMEM(weights.shape, weights.dtype),
            pltpu.VMEM((rows, levels, points), F32),
            pltpu.VMEM((rows + 2, depth, points), F32),
            pltpu.VMEM((groups, levels, points), F32),
            pltpu.VMEM(west.shape, F32),
            pltpu.VMEM(east.shape, F32),
            pltpu.VMEM(own.shape, F32),
            pltpu.SemaphoreType.DMA((4,)),
            pltpu.SemaphoreType.DMA((rows // 16,)),
            pltpu.SemaphoreType.DMA((rows // 16,)),
            pltpu.SemaphoreType.DMA((rows // 32,)),
        ],
        cost_estimate=pl.CostEstimate(flops=20000000000, bytes_accessed=16000000, transcendentals=0),
        compiler_params=params(22),
        name="prepare",
    )(place, info, *[in_hbm(x) for x in (moved, weights, west, east, own)])


def basis_kernel(
    info_ref, above_hbm, below_hbm, begun_hbm, strips_hbm, stiffness_hbm, ends_ref, smooth_ref,
    t0, t1, t2, t3, t4, past_ref, caps_ref, moments_ref,
    held, slope_ref, wide, polar_strips, side, side_slope, above_ref, below_ref, sems,
):
    rows, levels, points = slope_ref.shape
    depth = 3 * levels
    polar = caps_ref.shape[0]
    groups = rows // FIELDS
    table = [t0, t1, t2, t3, t4]
    start, is_polar = info_ref[0], info_ref[1]
    top, bottom = info_ref[2].astype(F32), info_ref[3].astype(F32)
    stride = 128
    first, last = FIELDS, FIELDS + rows - 1
    loads = [
        pltpu.make_async_copy(strips_hbm, held.at[:, pl.ds(1, groups)], sems.at[0]),
        pltpu.make_async_copy(begun_hbm, t0.at[pl.ds(first, rows)], sems.at[1]),
        pltpu.make_async_copy(stiffness_hbm, slope_ref, sems.at[2]),
    ]
    halo = [
        pltpu.make_async_copy(above_hbm, above_ref, sems.at[3]),
        pltpu.make_async_copy(below_hbm, below_ref, sems.at[4]),
    ]
    for load in halo + loads:
        load.start()
    difference = shift_matrix(points, -0.5, 0.5)
    neighbours = shift_matrix(points, 1.0, 1.0)
    half_sign = jnp.where(lanes((1, 1, points)) == 0, 0.5, -0.5)

    def component(x, which):
        return x[..., which * levels : (which + 1) * levels, :]

    def rhs(u, theta, north, south, inserted):
        return theta - (shifted(u, difference) - half_sign * inserted + 0.5 * (south - north))

    for load in halo:
        load.wait()
    nearest = []
    for end, ref in enumerate((above_ref, below_ref)):
        group = 0 if end == 0 else groups + 1
        left, right = ref[FIELDS], ref[FIELDS + 1]
        held[0, group], held[1, group] = left, right
        packed = beyond(left[0:levels], right[0:levels])[None]
        fields = ref[0:FIELDS, 0:depth]
        v = component(fields, 1)
        low, count = (FIELDS - ITERS, ITERS) if end == 0 else (0, ITERS)
        if end == 0:
            north = v[low - 1 : FIELDS - 1]
            south = jnp.concatenate([v[low + 1 :], ends_ref[0:1]], axis=0)
            nearest.append(0.5 * v[FIELDS - 1 :])
        else:
            north = jnp.concatenate([ends_ref[1:2], v[0 : count - 1]], axis=0)
            south = v[1 : count + 1]
            nearest.append(0.5 * v[0:1])
        value = rhs(
            component(fields, 0)[low : low + count], component(fields, 2)[low : low + count], north, south,
            insertions(packed, low, count),
        )
        place = first - FIELDS + low if end == 0 else last + 1
        t0[place : place + count] = (top if end == 0 else bottom) * value
    loads[0].wait()
    loads[1].wait()
    t0[first : first + 1] = t0[first : first + 1] + nearest[0]
    t0[last : last + 1] = t0[last : last + 1] - nearest[1]

    @pl.when(is_polar == 1)
    def _():
        half = depth // 2
        zero = jnp.zeros((1, depth, points), F32)
        wide[0:1] = zero
        wide[polar + 1 :] = zero
        shape = (depth, points)
        field = lanes(shape) // FIELD
        low = low_half(jnp.zeros(shape, F32))
        for group in range(polar // FIELDS):
            own, outer = jnp.zeros(shape, F32), jnp.zeros(shape, F32)
            for f in range(FIELDS):
                i = group * FIELDS + f
                lines = [smooth_ref[2 * i], smooth_ref[2 * i + 1]]
                row = jnp.concatenate([line[0:half] for line in lines], axis=0)
                caps_ref[i] = row
                wide[1 + i] = row
                edges = [shift(line[half:], FIELD * (f - t)) for line in lines for t in range(half // 8)]
                own = jnp.where(field == f, shift(row, FIELD * f + 8), own)
                outer = jnp.where(field == f, jnp.concatenate(edges, axis=0), outer)
            left, right = jnp.where(low, outer, own), jnp.where(low, own, outer)
            place = 1 + start // FIELDS + group
            held[0, place, 0:depth] = left
            held[1, place, 0:depth] = right
            polar_strips[group] = beyond(left[0:levels], right[0:levels])
        u, v, theta = [component(wide[...], which) for which in range(3)]
        here = pl.ds(first + start, polar)
        t0[here] = t0[here] + rhs(
            u[1:-1], theta[1:-1], v[:-2], v[2:], insertions(polar_strips[...], 0, polar)
        )

        @pl.when(start == 0)
        def _():
            e = first + polar
            t0[e : e + 1] = t0[e : e + 1] + 0.5 * v[polar : polar + 1]

        @pl.when(start != 0)
        def _():
            e = last - polar
            t0[e : e + 1] = t0[e : e + 1] - 0.5 * v[1:2]

    def beside_rows(x):
        lane = lanes(x.shape)
        down, up = shift(x, FIELD), shift(x, -FIELD)
        before = jnp.concatenate([down[:, :1], down[:, :-1]], axis=1)
        after = jnp.concatenate([up[:, 1:], up[:, -1:]], axis=1)
        return jnp.where(lane < FIELD, before, down), jnp.where(lane >= 128 - FIELD, after, up)

    def masked(x):
        return jnp.concatenate([top * x[:, :1], x[:, 1:-1], bottom * x[:, -1:]], axis=1)

    def keep(k, x):
        side[k] = x
        past_ref[k] = beyond(x[0], x[1])

    u = held[:, :, 0:levels]
    north, south = beside_rows(held[:, :, levels : 2 * levels])
    keep(0, masked(
        held[:, :, 2 * levels : depth] - 0.5 * (shift(u, -1) - shift(u, 1) + (south - north))
    ))
    side_slope[...] = (4.0 / 9.0) * (held[:, :, depth:] - 0.5)
    for k in range(ITERS - 1):
        here = side[k]
        north, south = beside_rows(here)
        twice = side_slope[...] * here - (4.0 / 9.0) * (shift(here, 1) + shift(here, -1) + (north + south))
        keep(k + 1, masked(0.5 * twice if k == 0 else twice - side[k - 1]))

    loads[2].wait()
    sums = []
    for k in range(ITERS):
        now = table[k]

        def following(e, count, stiff, inserted):
            here = now[pl.ds(e, count)]
            beside = shifted(here, neighbours) + inserted + (now[pl.ds(e - 1, count)] + now[pl.ds(e + 1, count)])
            twice = (4.0 / 9.0) * ((stiff - 0.5) * here - beside)
            if k == 0:
                return here, 0.5 * twice
            return here, twice - table[k - 1][pl.ds(e, count)]

        def step(i, carry):
            squares, cross = carry
            e = FIELDS + i * stride
            packed = past_ref[k, pl.ds(1 + i * (stride // FIELDS), stride // FIELDS)]
            here, value = following(e, stride, slope_ref[pl.ds(i * stride, stride)], insertions(packed, 0, stride))
            if k < ITERS - 1:
                table[k + 1][pl.ds(e, stride)] = value
            return squares + jnp.sum(here * here, axis=0), cross + jnp.sum(here * value, axis=0)

        zero = jnp.zeros((levels, points), F32)
        sums.append(lax.fori_loop(0, rows // stride, step, (zero, zero)))
        if k < ITERS - 1:
            reach = ITERS - 1 - k
            table[k + 1][first - reach : first] = top * following(
                first - reach, reach, above_ref[FIELDS - reach : FIELDS, depth:],
                insertions(past_ref[k, 0:1], FIELDS - reach, reach),
            )[1]
            table[k + 1][last + 1 : last + 1 + reach] = bottom * following(
                last + 1, reach, below_ref[0:reach, depth:], insertions(past_ref[k, groups + 1 :], 0, reach)
            )[1]

    lane = lanes((1, points))
    moments = jnp.zeros((1, points), F32)
    for i, value in enumerate([a for a, _ in sums] + [b for _, b in sums]):
        total = jnp.sum(jnp.sum(value, axis=0, keepdims=True), axis=1, keepdims=True)
        moments = jnp.where(lane == i, total, moments)
    moments_ref[...] = jnp.broadcast_to(moments, moments_ref.shape)


def make_basis(info, above, below, begun, sides, stiffness, ends, smooth, polar, devices):
    rows, levels, points = stiffness.shape
    depth = 3 * levels
    groups = rows // FIELDS + 2
    both = depth + levels
    vmem = pl.BlockSpec(memory_space=pltpu.VMEM)
    return pl.pallas_call(
        basis_kernel,
        in_specs=[pl.BlockSpec(memory_space=pltpu.SMEM)] + [pl.BlockSpec(memory_space=pl.ANY)] * 5 + [vmem] * 2,
        out_specs=(vmem,) * (ITERS + 3),
        out_shape=(pltpu.VMEM((rows + 2 * FIELDS, levels, points), F32),) * ITERS
        + (
            pltpu.VMEM((ITERS, groups, levels, points), F32),
            pltpu.HBM((polar, depth, points), F32),
            jax.ShapeDtypeStruct((devices, points), F32),
        ),
        scratch_shapes=[
            pltpu.VMEM((2, groups, both, points), F32),
            pltpu.VMEM(stiffness.shape, F32),
            pltpu.VMEM((polar + 2, depth, points), F32),
            pltpu.VMEM((polar // FIELDS, levels, points), F32),
            pltpu.VMEM((ITERS, 2, groups, levels, points), F32),
            pltpu.VMEM((2, groups, levels, points), F32),
            pltpu.VMEM(above.shape, F32),
            pltpu.VMEM(below.shape, F32),
            pltpu.SemaphoreType.DMA((5,)),
        ],
        cost_estimate=pl.CostEstimate(flops=40000000, bytes_accessed=24000000, transcendentals=0),
        compiler_params=params(16),
        name="basis",
    )(info, *[in_hbm(x) for x in (above, below, begun, sides, stiffness)], ends, smooth)


def solve(mu):
    gram = [[0.5 * (mu[i + j] + mu[abs(i - j)]) for j in range(ITERS + 1)] for i in range(ITERS)]

    def inner(a, b):
        return tree([x * tree([y * gram[i][j] for j, y in enumerate(b)]) for i, x in enumerate(a)])

    def image_of(a):
        out = [4.5 * x for x in a] + [jnp.zeros_like(a[0])]
        for k, x in enumerate(a):
            out[k + 1] = out[k + 1] + 2.25 * x
            out[abs(k - 1)] = out[abs(k - 1)] + 2.25 * x
        return out

    zero = jnp.zeros_like(mu[0])
    phi = []
    residual = [zero + 1.0]
    direction = residual
    norm = mu[0]
    for step in range(ITERS):
        image = image_of(direction)
        alpha = norm / inner(direction, image)
        phi = [x + alpha * y for x, y in zip(phi + [zero], direction)]
        if step < ITERS - 1:
            residual = [x - alpha * y for x, y in zip(residual + [zero], image)]
            following = inner(residual, residual)
            ratio = following / norm
            direction = [x + ratio * y for x, y in zip(residual, direction + [zero])]
            norm = following
    return phi


def finish_kernel(
    info_ref, spread_ref, filtered_hbm, caps_hbm, t0, t1, t2, t3, t4, past_ref, out_ref,
    coefficient_ref, filtered_ref, caps_ref, sems,
):
    table = [t0, t1, t2, t3, t4]
    _, levels, points = t0.shape
    block = out_ref.shape[0]
    g = pl.program_id(0)

    def fetch(i):
        part = pl.ds(i * block, block)
        return pltpu.make_async_copy(filtered_hbm.at[part], filtered_ref.at[part], sems.at[i])

    polar = caps_ref.shape[0]
    start, is_polar = info_ref[0], info_ref[1]
    fetch_caps = pltpu.make_async_copy(caps_hbm, caps_ref, sems.at[filtered_ref.shape[0] // block])

    @pl.when(g == 0)
    def _():
        fetch_caps.start()
        for i in range(filtered_ref.shape[0] // block):
            fetch(i).start()
        total = jnp.sum(spread_ref[...], axis=0, keepdims=True)
        lane = lanes(total.shape)
        picked = [
            jnp.sum(jnp.where(lane == i, total, 0.0), axis=1, keepdims=True) for i in range(2 * ITERS)
        ]
        mu = [picked[0], picked[ITERS]]
        for k in range(1, ITERS):
            mu += [2.0 * picked[k] - mu[0], 2.0 * picked[ITERS + k] - mu[1]]
        for k, value in enumerate(solve(mu)):
            coefficient_ref[k] = jnp.broadcast_to(value, (8, points))

    c = [jnp.concatenate([coefficient_ref[k]] * (levels // 8), axis=0) for k in range(ITERS)]

    fetch(g).wait()

    @pl.when(g == 0)
    def _():
        fetch_caps.wait()

    @pl.when((is_polar == 1) & (g == start // block))
    def _():
        filtered_ref[pl.ds(start, polar)] = caps_ref[...]

    def phi_of(e):
        return tree([c[k] * table[k][e] for k in range(ITERS)])

    lane = lanes((levels, points))
    stride = FIELDS

    def step(i, carry):
        first = i * stride
        row = g * block + first
        near = list(carry) + [phi_of(FIELDS + row + 1 + j) for j in range(stride)]
        packed = tree([c[k] * past_ref[k, 1 + row // FIELDS] for k in range(ITERS)])
        old = [filtered_ref[row + j] for j in range(stride)]
        new = []
        for j in range(stride):
            here = near[j + 1]
            inserted = unpack_lanes(packed, j)
            east = jnp.where(lane == points - 1, inserted, shift(here, -1))
            west = jnp.where(lane == 0, inserted, shift(here, 1))
            new.append(old[j][0:levels] - 0.5 * (east - west))
            new.append(old[j][levels : 2 * levels] - 0.5 * (near[j + 2] - near[j]))
            new.append(old[j][2 * levels :] - here)
        for j in range(stride):
            for part in range(3):
                out_ref[first + j, part * levels : (part + 1) * levels] = new[3 * j + part]
        return near[stride], near[stride + 1]

    e = FIELDS + g * block
    lax.fori_loop(0, block // stride, step, (phi_of(e - 1), phi_of(e)))


def finish(info, spread, filtered, caps, table):
    rows, depth, points = filtered.shape
    block = 32
    vmem = pl.BlockSpec(memory_space=pltpu.VMEM)
    piece = pl.BlockSpec((block, depth, points), lambda g: (g, 0, 0))
    return pl.pallas_call(
        finish_kernel,
        grid=(rows // block,),
        in_specs=[pl.BlockSpec(memory_space=pltpu.SMEM), vmem] + [pl.BlockSpec(memory_space=pl.ANY)] * 2 + [vmem] * (ITERS + 1),
        out_specs=piece,
        out_shape=jax.ShapeDtypeStruct((rows, depth, points), F32),
        scratch_shapes=[
            pltpu.VMEM((ITERS, 8, points), F32),
            pltpu.VMEM((rows, depth, points), F32),
            pltpu.VMEM(caps.shape, F32),
            pltpu.SemaphoreType.DMA((rows // block + 1,)),
        ],
        cost_estimate=pl.CostEstimate(flops=20000000, bytes_accessed=17000000, transcendentals=0),
        compiler_params=params(12),
        name="finish",
    )(info, spread, in_hbm(filtered), in_hbm(caps), *table)


def shards(state, weights, owners, source_rows, cutoffs, stiffness):
    rows, comps, levels, points = state.shape
    depth = comps * levels
    n_lon = lax.axis_size("lon")
    n_lat = lax.axis_size("lat")
    devices = n_lon * n_lat
    band = lax.axis_index("lat")
    north, south = band == 0, band == n_lat - 1
    polar = cutoffs.shape[0] // 2
    line = lax.axis_index("lon") * polar // n_lon
    info = jnp.stack(
        [
            jnp.where(north, 0, rows - polar),
            (north | south).astype(jnp.int32),
            (band > 0).astype(jnp.int32),
            (band < n_lat - 1).astype(jnp.int32),
            cutoffs[jnp.where(north, line, polar + line)],
        ]
    ).astype(jnp.int32)

    requests, place = make_requests(owners[:, :, 0], source_rows)
    asked = exchange(requests, BOTH)[:, :2]
    asked, ahead, ahead_weights = lax.optimization_barrier((asked, stiffness, weights))
    moved = exchange(state[asked], BOTH).reshape(2 * devices, depth, points)
    moved, rim_weights, *stiff = lax.optimization_barrier(
        (moved, edge_weights(ahead_weights)) + tuple(pack_stiffness(ahead))
    )

    place = place[0]
    caps, last, first = make_caps(place, info, moved, weights, stiffness, polar)
    lines = exchange(caps.reshape(n_lon, -1, points), "lon")
    place, caps = lax.optimization_barrier((place, caps))
    to_east, to_west, own = make_edges(place, moved, rim_weights, stiff)
    west, east = from_sides(to_east, to_west)
    passed = low_pass(info, lines)
    smooth = exchange(passed, "lon")
    _, west_late, east_late = lax.optimization_barrier((passed, west, east))
    above, below = from_ends(*make_ends(last, first, west_late, east_late))
    arrived, begun, sides, near = prepare(place, info, moved, weights, west, east, own)
    *table, caps, moments = make_basis(info, above, below, begun, sides, stiffness, near, smooth, polar, devices)
    out = finish(info, exchange(moments, BOTH), arrived, caps, table)
    return out.reshape(rows, comps, levels, points)


def solution(mesh):
    in_specs = (
        P("lat", None, None, "lon"),
        P("lat", None, "lon"),
        P("lon", "lat", None),
        P("lon", "lat"),
        P(),
        P("lat", None, "lon"),
    )
    out_specs = P("lat", None, None, "lon")
    return jax.shard_map(shards, mesh=mesh, in_specs=in_specs, out_specs=out_specs, check_vma=False)
```

```python
import functools

import numpy as np
import jax
import jax.numpy as jnp
from jax import lax
from jax.experimental import pallas as pl
from jax.experimental.pallas import tpu as pltpu
from jax.sharding import PartitionSpec as P

ITERS = 5
BOTH = ("lon", "lat")
HIGHEST = lax.Precision.HIGHEST
FIELD = 16
FIELDS = 8
F32 = jnp.float32
MIB = 1024 * 1024


def params(mib):
    return pltpu.CompilerParams(vmem_limit_bytes=mib * MIB)


def in_hbm(x):
    return pltpu.with_memory_space_constraint(x, pltpu.HBM)


def exchange(block, axes):
    return lax.all_to_all(block, axes, split_axis=0, concat_axis=0, tiled=True)


def lanes(shape):
    return lax.broadcasted_iota(jnp.int32, shape, len(shape) - 1)


def pack_lanes(shape, rows):
    field = lanes(shape) // FIELD
    packed = jnp.zeros(shape, F32)
    for f, row in enumerate(rows):
        packed = jnp.where(field == f, pltpu.roll(row, (FIELD * f + 8) % 128, len(shape) - 1), packed)
    return packed


def unpack_lanes(packed, f):
    return pltpu.roll(packed, (-(FIELD * f + 8)) % 128, packed.ndim - 1)


def request_kernel(row_ref, wanted_ref, request_ref, place_ref):
    row = row_ref[...]
    size = row.shape[1]
    down = lax.broadcasted_iota(jnp.int32, (size, size), 0)
    across = lax.broadcasted_iota(jnp.int32, (size, size), 1)
    owner = jnp.broadcast_to(row, (size, size))
    earlier = (owner.T == owner) & (down < across)
    slot = jnp.sum(jnp.where(earlier, 1.0, 0.0), axis=0, keepdims=True)
    wanted = wanted_ref[...].astype(F32)
    out = jnp.zeros((size, size), F32)
    for s in range(2):
        hit = jnp.where((owner == down) & (slot == s), wanted, 0.0)
        out = jnp.where(across == s, jnp.sum(hit, axis=1, keepdims=True), out)
    request_ref[...] = out.astype(jnp.int32)
    place_ref[...] = 2 * row + slot.astype(jnp.int32)


def make_requests(owner, wanted):
    rows = wanted.shape[1]
    return pl.pallas_call(
        request_kernel,
        out_shape=(
            jax.ShapeDtypeStruct((rows, rows), jnp.int32),
            jax.ShapeDtypeStruct((1, rows), jnp.int32),
        ),
        cost_estimate=pl.CostEstimate(flops=200000, bytes_accessed=200000, transcendentals=0),
        compiler_params=params(2),
        name="requests",
    )(in_hbm(owner), in_hbm(wanted))


def ways(axis, wrap):
    count = lax.axis_size(axis)
    up = [(i, (i + 1) % count) for i in range(count if wrap else count - 1)]
    return up, [(b, a) for a, b in up]


def from_sides(to_east, to_west):
    east, west = ways("lon", True)
    return lax.ppermute(to_east, "lon", east), lax.ppermute(to_west, "lon", west)


def from_ends(last, first):
    north, south = ways("lat", False)
    return lax.ppermute(last, "lat", north), lax.ppermute(first, "lat", south)


def low_half(x):
    return lanes(x.shape) % FIELD < FIELD // 2


def shift(x, by):
    return pltpu.roll(x, by % 128, x.ndim - 1)


def for_sides(even, odd):
    low = low_half(even)
    return jnp.where(low, even, shift(odd, 8)), jnp.where(low, shift(even, -8), odd)


def strips(from_west, from_east, own, parity):
    low = low_half(own)
    if parity == 0:
        return jnp.where(low, from_west, own), jnp.where(low, own, shift(from_east, 8))
    return jnp.where(low, shift(from_west, -8), own), jnp.where(low, own, from_east)


def beyond(left, right):
    return jnp.where(lanes(left.shape) % FIELD == FIELD // 2, shift(left, 1), shift(right, -1))


def insertion(packed, f):
    lane = lanes(packed.shape)
    return jnp.where((lane == 0) | (lane == 127), unpack_lanes(packed, f), 0.0)


def insertions(packed, first, count):
    return jnp.stack([insertion(packed[(first + i) // FIELDS], (first + i) % FIELDS) for i in range(count)])


def caps_kernel(
    place_ref, info_ref, moved_hbm, weights_hbm, stiffness_hbm, caps_ref, last_ref, first_ref,
    held, weights_ref, stiffness_ref, row_sems, sems,
):
    polar = caps_ref.shape[0]
    depth = caps_ref.shape[1]
    rows = weights_hbm.shape[0]
    start = info_ref[0]
    spans = [(start, 0, polar), (0, polar, FIELDS), (rows - FIELDS, polar + FIELDS, FIELDS)]
    copies = []
    for n, (row, at, count) in enumerate(spans):
        copies.append(
            pltpu.make_async_copy(weights_hbm.at[pl.ds(row, count)], weights_ref.at[pl.ds(at, count)], sems.at[n])
        )
        copies += [
            pltpu.make_async_copy(moved_hbm.at[place_ref[row + i]], held.at[at + i], row_sems.at[at + i])
            for i in range(count)
        ]
    for end, row in enumerate((0, rows - FIELDS)):
        copies.append(
            pltpu.make_async_copy(stiffness_hbm.at[pl.ds(row, FIELDS)], stiffness_ref.at[end], sems.at[3 + end])
        )
    for copy in copies:
        copy.start()
    for copy in copies:
        copy.wait()
    values = [
        jnp.dot(held[i], weights_ref[i], preferred_element_type=F32) for i in range(polar + 2 * FIELDS)
    ]
    for i in range(polar):
        caps_ref[i] = values[i]
    for end, ref in enumerate((first_ref, last_ref)):
        low = polar + end * FIELDS
        rim = values[low : low + FIELDS]
        stiff = [stiffness_ref[end, f] for f in range(FIELDS)]
        for f in range(FIELDS):
            ref[f, 0:depth] = rim[f]
            ref[f, depth:] = stiff[f]
        ref[FIELDS, 0:depth] = pack_lanes(rim[0].shape, rim)
        ref[FIELDS, depth:] = pack_lanes(stiff[0].shape, stiff)


def make_caps(place, info, moved, weights, stiffness, polar):
    _, depth, points = moved.shape
    levels = stiffness.shape[1]
    smem = pl.BlockSpec(memory_space=pltpu.SMEM)
    hbm = pl.BlockSpec(memory_space=pl.ANY)
    count = polar + 2 * FIELDS
    rim = jax.ShapeDtypeStruct((FIELDS + 1, depth + levels, points), F32)
    return pl.pallas_call(
        caps_kernel,
        in_specs=[smem, smem, hbm, hbm, hbm],
        out_specs=[pl.BlockSpec(memory_space=pltpu.VMEM)] * 3,
        out_shape=(jax.ShapeDtypeStruct((polar, depth, points), F32), rim, rim),
        scratch_shapes=[
            pltpu.VMEM((count, depth, points), moved.dtype),
            pltpu.VMEM((count, points, points), weights.dtype),
            pltpu.VMEM((2, FIELDS, levels, points), F32),
            pltpu.SemaphoreType.DMA((count,)),
            pltpu.SemaphoreType.DMA((5,)),
        ],
        cost_estimate=pl.CostEstimate(flops=60000000, bytes_accessed=2400000, transcendentals=0),
        compiler_params=params(6),
        name="caps",
    )(place, info, in_hbm(moved), in_hbm(weights), in_hbm(stiffness))


def stiff_kernel(stiffness_ref, east_ref, west_ref, own_ref):
    def pair(g, carry):
        packed = []
        for h in range(2):
            rows = [stiffness_ref[(2 * g + h) * FIELDS + f] for f in range(FIELDS)]
            packed.append(pack_lanes(rows[0].shape, rows))
        east_ref[g], west_ref[g] = for_sides(*packed)
        own_ref[2 * g], own_ref[2 * g + 1] = packed
        return carry

    lax.fori_loop(0, east_ref.shape[0], pair, 0)


def pack_stiffness(stiffness):
    rows, levels, points = stiffness.shape
    side = pltpu.HBM((rows // (2 * FIELDS), levels, points), F32)
    return pl.pallas_call(
        stiff_kernel,
        out_shape=(side, side, pltpu.HBM((rows // FIELDS, levels, points), F32)),
        cost_estimate=pl.CostEstimate(flops=1000000, bytes_accessed=1300000, transcendentals=0),
        compiler_params=params(4),
        name="pack_stiffness",
    )(in_hbm(stiffness))


def edge_weights_kernel(weights_ref, out_ref):
    rows = [weights_ref[f].astype(F32) for f in range(FIELDS)]
    out_ref[0] = pack_lanes(rows[0].shape, rows).astype(out_ref.dtype)


def edge_weights(weights):
    rows, points, _ = weights.shape
    return pl.pallas_call(
        edge_weights_kernel,
        grid=(rows // FIELDS,),
        in_specs=[pl.BlockSpec((FIELDS, points, points), lambda g: (g, 0, 0))],
        out_specs=pl.BlockSpec((1, points, points), lambda g: (g, 0, 0)),
        out_shape=pltpu.HBM((rows // FIELDS, points, points), weights.dtype),
        cost_estimate=pl.CostEstimate(flops=2000000, bytes_accessed=5000000, transcendentals=0),
        compiler_params=params(6),
        name="edge_weights",
    )(in_hbm(weights))


def edges_kernel(
    place_ref, moved_hbm, east_hbm, west_hbm, own_hbm, weights_hbm, east_ref, west_ref, own_ref,
    moved_ref, weights_ref, sems,
):
    depth = moved_ref.shape[1]
    levels = own_hbm.shape[1]
    loads = [
        pltpu.make_async_copy(moved_hbm, moved_ref, sems.at[0]),
        pltpu.make_async_copy(weights_hbm, weights_ref, sems.at[1]),
        pltpu.make_async_copy(east_hbm, east_ref.at[:, pl.ds(depth, levels)], sems.at[2]),
        pltpu.make_async_copy(west_hbm, west_ref.at[:, pl.ds(depth, levels)], sems.at[3]),
        pltpu.make_async_copy(own_hbm, own_ref.at[:, pl.ds(depth, levels)], sems.at[4]),
    ]
    for load in loads:
        load.start()
    for load in loads[:2]:
        load.wait()
    shape = (depth, moved_ref.shape[2])
    field = lanes(shape) // FIELD

    def pair(g, carry):
        packed = []
        for h in range(2):
            group = 2 * g + h
            sources = [moved_ref[place_ref[group * FIELDS + f]] for f in range(FIELDS)]
            product = jnp.dot(
                jnp.concatenate(sources, axis=0), weights_ref[group], preferred_element_type=F32
            )
            value = jnp.zeros(shape, F32)
            for f in range(FIELDS):
                value = jnp.where(field == f, product[f * depth : (f + 1) * depth], value)
            packed.append(value)
        east, west = for_sides(*packed)
        east_ref[g, 0:depth] = east
        west_ref[g, 0:depth] = west
        for h in range(2):
            own_ref[2 * g + h, 0:depth] = packed[h]
        return carry

    lax.fori_loop(0, east_ref.shape[0], pair, 0, unroll=True)
    for load in loads[2:]:
        load.wait()


def make_edges(place, moved, weights, stiff):
    _, depth, points = moved.shape
    groups, levels, _ = stiff[2].shape
    both = depth + levels
    vmem = pl.BlockSpec(memory_space=pltpu.VMEM)
    hbm = pl.BlockSpec(memory_space=pl.ANY)
    side = jax.ShapeDtypeStruct((groups // 2, both, points), F32)
    return pl.pallas_call(
        edges_kernel,
        in_specs=[pl.BlockSpec(memory_space=pltpu.SMEM)] + [hbm] * 5,
        out_specs=[vmem] * 3,
        out_shape=(side, side, pltpu.HBM((groups, both, points), F32)),
        scratch_shapes=[
            pltpu.VMEM(moved.shape, moved.dtype),
            pltpu.VMEM(weights.shape, weights.dtype),
            pltpu.SemaphoreType.DMA((5,)),
        ],
        cost_estimate=pl.CostEstimate(flops=10000000000, bytes_accessed=5000000, transcendentals=0),
        compiler_params=params(10),
        name="edges",
    )(place, in_hbm(moved), *[in_hbm(x) for x in stiff], in_hbm(weights))


def ends_kernel(last_rim_ref, first_rim_ref, west_ref, east_ref, last_ref, first_ref):
    pairs = west_ref.shape[0]
    for rim, ref, end, pair in ((first_rim_ref, first_ref, 0, 0), (last_rim_ref, last_ref, 1, pairs - 1)):
        ref[0:FIELDS] = rim[0:FIELDS]
        ref[FIELDS], ref[FIELDS + 1] = strips(west_ref[pair], east_ref[pair], rim[FIELDS], end)


def make_ends(last, first, west, east):
    _, both, points = last.shape
    shape = jax.ShapeDtypeStruct((FIELDS + 2, both, points), F32)
    return pl.pallas_call(
        ends_kernel,
        out_shape=(shape, shape),
        cost_estimate=pl.CostEstimate(flops=100000, bytes_accessed=2000000, transcendentals=0),
        compiler_params=params(6),
        name="ends",
    )(last, first, west, east)


def tree(terms):
    while len(terms) > 1:
        terms = [a + b for a, b in zip(terms[::2], terms[1::2])] + terms[len(terms) // 2 * 2 :]
    return terms[0]


def halves(table):
    high = table.astype(jnp.bfloat16)
    return np.stack([high, (table - high.astype(np.float64)).astype(jnp.bfloat16)])


def filter_tables(parts, points):
    total = parts * points
    half = parts // 2 + 1
    k1, p = np.arange(half), np.arange(points)
    twist = 2 * np.pi * np.outer(k1, p) / total
    inner = 2 * np.pi * np.outer(p, p) / points
    c, s = np.cos(inner), np.sin(inner)
    forward = np.block([[c, -s], [s, c]])
    inverse = np.block([[c, s], [-s, c]])
    twist = np.concatenate([np.cos(twist), np.sin(twist)]).astype(np.float32)
    return twist, halves(forward), halves(inverse)


def cosine_sums(v, parts):
    mid, quarter = parts // 2, parts // 4
    plus = [v[j - 1] + v[mid - j - 1] for j in range(1, quarter)]
    minus = [v[j - 1] - v[mid - j - 1] for j in range(1, quarter)]
    out = []
    for m in range(mid + 1):
        folded = plus if m % 2 == 0 else minus
        terms = [float(np.cos(2 * np.pi * m * j / parts)) * folded[j - 1] for j in range(1, quarter)]
        if m % 2 == 0:
            terms.append(v[quarter - 1] if m % 4 == 0 else -v[quarter - 1])
        out.append(tree(terms))
    return out


def sine_sums(v, parts):
    mid, quarter = parts // 2, parts // 4
    plus = [v[j - 1] + v[mid - j - 1] for j in range(1, quarter)]
    minus = [v[j - 1] - v[mid - j - 1] for j in range(1, quarter)]
    out = []
    for m in range(1, mid):
        folded = minus if m % 2 == 0 else plus
        terms = [float(np.sin(2 * np.pi * m * j / parts)) * folded[j - 1] for j in range(1, quarter)]
        if m % 2 == 1:
            terms.append(v[quarter - 1] if m % 4 == 1 else -v[quarter - 1])
        out.append(tree(terms))
    return out


def product(x, table_ref):
    high, low = split(x)
    count = x.shape[0]
    both = jnp.dot(jnp.concatenate([high, low], axis=0), table_ref[0], preferred_element_type=F32)
    return both[:count] + both[count:] + jnp.dot(high, table_ref[1], preferred_element_type=F32)


def filter_kernel(
    info_ref, lines_ref, twist_hbm, forward_hbm, inverse_hbm, out_ref,
    work, back, twist_ref, forward_ref, inverse_ref, sems,
):
    parts, count, points = lines_ref.shape
    pairs = [(twist_hbm, twist_ref), (forward_hbm, forward_ref), (inverse_hbm, inverse_ref)]
    loads = [pltpu.make_async_copy(a, b, sems.at[i]) for i, (a, b) in enumerate(pairs)]
    for load in loads:
        load.start()
    total = parts * points
    mid = parts // 2
    cutoff = info_ref[4]
    tiles = count // 8
    loads[0].wait()
    for t in range(tiles):
        x = [lines_ref[d, 8 * t : 8 * t + 8, :] for d in range(parts)]
        even = cosine_sums([x[d] + x[parts - d] for d in range(1, mid)], parts)
        odd = sine_sums([x[d] - x[parts - d] for d in range(1, mid)], parts)
        ends = (x[0] + x[mid], x[0] - x[mid])
        for k in range(mid + 1):
            real = ends[k % 2] + even[k]
            row = k * count + 8 * t
            tc, ts = twist_ref[k : k + 1, :], twist_ref[mid + 1 + k : mid + 2 + k, :]
            if k in (0, mid):
                work[row : row + 8, 0:points] = real * tc
                work[row : row + 8, points:] = -real * ts
            else:
                imag = odd[k - 1]
                work[row : row + 8, 0:points] = real * tc - imag * ts
                work[row : row + 8, points:] = -imag * tc - real * ts
    loads[1].wait()
    spectrum = product(work[...], forward_ref)
    shape = spectrum.shape
    wave = lax.broadcasted_iota(jnp.int32, shape, 0) // count + parts * (lanes(shape) % points)
    kept = (wave <= cutoff) | (wave >= total - cutoff)
    spectrum = jnp.where(kept, spectrum * (1.0 / total), 0.0)
    loads[2].wait()
    back[...] = product(spectrum, inverse_ref)
    for t in range(tiles):
        real, imag = [], []
        for k in range(mid + 1):
            row = k * count + 8 * t
            br, bi = back[row : row + 8, 0:points], back[row : row + 8, points:]
            tc, ts = twist_ref[k : k + 1, :], twist_ref[mid + 1 + k : mid + 2 + k, :]
            real.append(br * tc - bi * ts)
            if k not in (0, mid):
                imag.append(br * ts + bi * tc)
        even = cosine_sums(real[1:mid], parts)
        odd = sine_sums(imag, parts)
        ends = (real[0] + real[mid], real[0] - real[mid])
        for d in range(mid + 1):
            value = ends[d % 2] + 2.0 * even[d]
            if d in (0, mid):
                out_ref[d, 8 * t : 8 * t + 8, :] = value
            else:
                out_ref[d, 8 * t : 8 * t + 8, :] = value - 2.0 * odd[d - 1]
                out_ref[parts - d, 8 * t : 8 * t + 8, :] = value + 2.0 * odd[d - 1]
    shape = (8, points)
    low = lanes(shape) < points // 2
    for d in range(parts):
        rows = [
            jnp.where(
                low,
                out_ref[(d + 1) % parts, 8 * t : 8 * t + 8, :],
                out_ref[(d - 1) % parts, 8 * t : 8 * t + 8, :],
            )
            for t in range(tiles)
        ]
        out_ref[d, count : count + 8, :] = pack_lanes(shape, rows)


def low_pass(info, lines):
    parts, count, points = lines.shape
    tables = filter_tables(parts, points)
    rows = (parts // 2 + 1) * count
    vmem = pl.BlockSpec(memory_space=pltpu.VMEM)
    return pl.pallas_call(
        filter_kernel,
        in_specs=[pl.BlockSpec(memory_space=pltpu.SMEM)] + [vmem] + [pl.BlockSpec(memory_space=pl.ANY)] * 3,
        out_specs=vmem,
        out_shape=pltpu.HBM((parts, count + 8, points), F32),
        scratch_shapes=[pltpu.VMEM((rows, 2 * points), F32)] * 2
        + [pltpu.VMEM(x.shape, x.dtype) for x in tables]
        + [pltpu.SemaphoreType.DMA((3,))],
        cost_estimate=pl.CostEstimate(flops=700000000, bytes_accessed=1400000, transcendentals=0),
        compiler_params=params(8),
        name="low_pass",
    )(info, lines, *[in_hbm(jnp.asarray(x)) for x in tables])


def split(x):
    high = x.astype(jnp.bfloat16)
    return high, (x - high.astype(F32)).astype(jnp.bfloat16)


def shift_matrix(points, left, right):
    source = lax.broadcasted_iota(jnp.int32, (2 * points, points), 0) % points
    target = lax.broadcasted_iota(jnp.int32, (2 * points, points), 1)
    west, east = source + 1 == target, source == target + 1
    return (jnp.where(west, left, 0.0) + jnp.where(east, right, 0.0)).astype(jnp.bfloat16)


def shifted(x, matrix):
    flat = x.reshape(-1, x.shape[-1])
    out = jnp.dot(jnp.concatenate(split(flat), axis=1), matrix, preferred_element_type=F32)
    return out.reshape(x.shape)


def prepare_kernel(
    place_ref, info_ref, moved_hbm, weights_hbm, west_hbm, east_hbm, own_hbm,
    arrived_hbm, begun_hbm, strips_ref, ends_ref,
    moved_ref, weights_ref, begun_ref, wide, past, west_ref, east_ref, own_ref, sems, weight_sems, row_sems, save_sems,
):
    rows, levels, points = begun_ref.shape
    depth = wide.shape[1]
    polar = 16
    pieces, stride = rows // polar, 2 * polar
    start, is_polar = info_ref[0], info_ref[1]
    pairs = [(west_hbm, west_ref), (east_hbm, east_ref), (own_hbm, own_ref), (moved_hbm, moved_ref)]
    loads = [pltpu.make_async_copy(a, b, sems.at[i]) for i, (a, b) in enumerate(pairs)]

    def fetch(i):
        piece = pl.ds(i * polar, polar)
        return pltpu.make_async_copy(weights_hbm.at[piece], weights_ref.at[piece], weight_sems.at[i])

    def save_rows(i):
        return pltpu.make_async_copy(
            wide.at[pl.ds(1 + i * polar, polar)], arrived_hbm.at[pl.ds(i * polar, polar)], row_sems.at[i]
        )

    def save(i):
        piece = pl.ds(i * stride, stride)
        return pltpu.make_async_copy(begun_ref.at[piece], begun_hbm.at[piece], save_sems.at[i])

    for load in loads:
        load.start()
    for i in range(pieces):
        fetch(i).start()
    zero = jnp.zeros((1, depth, points), F32)
    for row in (0, rows + 1):
        wide[row : row + 1] = zero
    for load in loads[:3]:
        load.wait()
    for g in range(rows // FIELDS):
        left, right = strips(west_ref[g // 2], east_ref[g // 2], own_ref[g], g % 2)
        strips_ref[0, g], strips_ref[1, g] = left, right
        past[g] = beyond(left[0:levels], right[0:levels])

    @pl.when(is_polar == 1)
    def _():
        past[pl.ds(start // FIELDS, polar // FIELDS)] = jnp.zeros((polar // FIELDS, levels, points), F32)

    loads[3].wait()
    difference = shift_matrix(points, -0.5, 0.5)
    half_sign = jnp.where(lanes((1, 1, points)) == 0, 0.5, -0.5)

    def interpolate(i):
        fetch(i).wait()
        first = i * polar
        sources = [moved_ref[place_ref[first + j]] for j in range(polar)]
        values = [
            jnp.dot(source, weights_ref[first + j], preferred_element_type=F32) for j, source in enumerate(sources)
        ]
        for j, value in enumerate(values):
            wide[1 + first + j] = value

        @pl.when((is_polar == 1) & (start // polar == i))
        def _():
            wide[1 + first : 1 + first + polar] = jnp.zeros((polar, depth, points), F32)

        save_rows(i).start()

    def step(i):
        e = 1 + i * stride
        part = lambda e, which: wide[pl.ds(e, stride), which * levels : (which + 1) * levels]
        groups = past[pl.ds(i * (stride // FIELDS), stride // FIELDS)]
        across = shifted(part(e, 0), difference) - half_sign * insertions(groups, 0, stride)
        begun_ref[pl.ds(i * stride, stride)] = part(e, 2) - (across + 0.5 * (part(e + 1, 1) - part(e - 1, 1)))
        save(i).start()

    for i in range(pieces):
        interpolate(i)
        if i % 2 == 0 and i > 0:
            step(i // 2 - 1)
    step(pieces // 2 - 1)
    ends_ref[0] = wide[1, levels : 2 * levels]
    ends_ref[1] = wide[rows, levels : 2 * levels]
    for i in range(pieces):
        save_rows(i).wait()
    for i in range(rows // stride):
        save(i).wait()


def prepare(place, info, moved, weights, west, east, own):
    rows, points, _ = weights.shape
    groups, both, _ = own.shape
    depth = moved.shape[1]
    levels = both - depth
    vmem = pl.BlockSpec(memory_space=pltpu.VMEM)
    hbm = pl.BlockSpec(memory_space=pl.ANY)
    return pl.pallas_call(
        prepare_kernel,
        in_specs=[pl.BlockSpec(memory_space=pltpu.SMEM)] * 2 + [hbm] * 5,
        out_specs=[hbm, hbm, vmem, vmem],
        out_shape=(
            pltpu.HBM((rows, depth, points), F32),
            pltpu.HBM((rows, levels, points), F32),
            pltpu.HBM((2, groups, both, points), F32),
            jax.ShapeDtypeStruct((2, levels, points), F32),
        ),
        scratch_shapes=[
            pltpu.VMEM(moved.shape, moved.dtype),
            pltpu.VMEM(weights.shape, weights.dtype),
            pltpu.VMEM((rows, levels, points), F32),
            pltpu.VMEM((rows + 2, depth, points), F32),
            pltpu.VMEM((groups, levels, points), F32),
            pltpu.VMEM(west.shape, F32),
            pltpu.VMEM(east.shape, F32),
            pltpu.VMEM(own.shape, F32),
            pltpu.SemaphoreType.DMA((4,)),
            pltpu.SemaphoreType.DMA((rows // 16,)),
            pltpu.SemaphoreType.DMA((rows // 16,)),
            pltpu.SemaphoreType.DMA((rows // 32,)),
        ],
        cost_estimate=pl.CostEstimate(flops=20000000000, bytes_accessed=16000000, transcendentals=0),
        compiler_params=params(22),
        name="prepare",
    )(place, info, *[in_hbm(x) for x in (moved, weights, west, east, own)])


def basis_kernel(
    info_ref, above_hbm, below_hbm, begun_hbm, strips_hbm, stiffness_hbm, ends_ref, smooth_ref,
    t0, t1, t2, t3, t4, past_ref, caps_ref, moments_ref,
    held, slope_ref, wide, polar_strips, side, side_slope, above_ref, below_ref, sems,
):
    rows, levels, points = slope_ref.shape
    depth = 3 * levels
    polar = caps_ref.shape[0]
    groups = rows // FIELDS
    table = [t0, t1, t2, t3, t4]
    start, is_polar = info_ref[0], info_ref[1]
    top, bottom = info_ref[2].astype(F32), info_ref[3].astype(F32)
    stride = 128
    first, last = FIELDS, FIELDS + rows - 1
    loads = [
        pltpu.make_async_copy(strips_hbm, held.at[:, pl.ds(1, groups)], sems.at[0]),
        pltpu.make_async_copy(begun_hbm, t0.at[pl.ds(first, rows)], sems.at[1]),
        pltpu.make_async_copy(stiffness_hbm, slope_ref, sems.at[2]),
    ]
    halo = [
        pltpu.make_async_copy(above_hbm, above_ref, sems.at[3]),
        pltpu.make_async_copy(below_hbm, below_ref, sems.at[4]),
    ]
    for load in halo + loads:
        load.start()
    difference = shift_matrix(points, -0.5, 0.5)
    neighbours = shift_matrix(points, 1.0, 1.0)
    half_sign = jnp.where(lanes((1, 1, points)) == 0, 0.5, -0.5)

    def component(x, which):
        return x[..., which * levels : (which + 1) * levels, :]

    def rhs(u, theta, north, south, inserted):
        return theta - (shifted(u, difference) - half_sign * inserted + 0.5 * (south - north))

    for load in halo:
        load.wait()
    nearest = []
    for end, ref in enumerate((above_ref, below_ref)):
        group = 0 if end == 0 else groups + 1
        left, right = ref[FIELDS], ref[FIELDS + 1]
        held[0, group], held[1, group] = left, right
        packed = beyond(left[0:levels], right[0:levels])[None]
        fields = ref[0:FIELDS, 0:depth]
        v = component(fields, 1)
        low, count = (FIELDS - ITERS, ITERS) if end == 0 else (0, ITERS)
        if end == 0:
            north = v[low - 1 : FIELDS - 1]
            south = jnp.concatenate([v[low + 1 :], ends_ref[0:1]], axis=0)
            nearest.append(0.5 * v[FIELDS - 1 :])
        else:
            north = jnp.concatenate([ends_ref[1:2], v[0 : count - 1]], axis=0)
            south = v[1 : count + 1]
            nearest.append(0.5 * v[0:1])
        value = rhs(
            component(fields, 0)[low : low + count], component(fields, 2)[low : low + count], north, south,
            insertions(packed, low, count),
        )
        place = first - FIELDS + low if end == 0 else last + 1
        t0[place : place + count] = (top if end == 0 else bottom) * value
    loads[0].wait()
    loads[1].wait()
    t0[first : first + 1] = t0[first : first + 1] + nearest[0]
    t0[last : last + 1] = t0[last : last + 1] - nearest[1]

    @pl.when(is_polar == 1)
    def _():
        half = depth // 2
        zero = jnp.zeros((1, depth, points), F32)
        wide[0:1] = zero
        wide[polar + 1 :] = zero
        shape = (depth, points)
        field = lanes(shape) // FIELD
        low = low_half(jnp.zeros(shape, F32))
        for group in range(polar // FIELDS):
            own, outer = jnp.zeros(shape, F32), jnp.zeros(shape, F32)
            for f in range(FIELDS):
                i = group * FIELDS + f
                lines = [smooth_ref[2 * i], smooth_ref[2 * i + 1]]
                row = jnp.concatenate([line[0:half] for line in lines], axis=0)
                caps_ref[i] = row
                wide[1 + i] = row
                edges = [shift(line[half:], FIELD * (f - t)) for line in lines for t in range(half // 8)]
                own = jnp.where(field == f, shift(row, FIELD * f + 8), own)
                outer = jnp.where(field == f, jnp.concatenate(edges, axis=0), outer)
            left, right = jnp.where(low, outer, own), jnp.where(low, own, outer)
            place = 1 + start // FIELDS + group
            held[0, place, 0:depth] = left
            held[1, place, 0:depth] = right
            polar_strips[group] = beyond(left[0:levels], right[0:levels])
        u, v, theta = [component(wide[...], which) for which in range(3)]
        here = pl.ds(first + start, polar)
        t0[here] = t0[here] + rhs(
            u[1:-1], theta[1:-1], v[:-2], v[2:], insertions(polar_strips[...], 0, polar)
        )

        @pl.when(start == 0)
        def _():
            e = first + polar
            t0[e : e + 1] = t0[e : e + 1] + 0.5 * v[polar : polar + 1]

        @pl.when(start != 0)
        def _():
            e = last - polar
            t0[e : e + 1] = t0[e : e + 1] - 0.5 * v[1:2]

    def beside_rows(x):
        lane = lanes(x.shape)
        down, up = shift(x, FIELD), shift(x, -FIELD)
        before = jnp.concatenate([down[:, :1], down[:, :-1]], axis=1)
        after = jnp.concatenate([up[:, 1:], up[:, -1:]], axis=1)
        return jnp.where(lane < FIELD, before, down), jnp.where(lane >= 128 - FIELD, after, up)

    def masked(x):
        return jnp.concatenate([top * x[:, :1], x[:, 1:-1], bottom * x[:, -1:]], axis=1)

    def keep(k, x):
        side[k] = x
        past_ref[k] = beyond(x[0], x[1])

    u = held[:, :, 0:levels]
    north, south = beside_rows(held[:, :, levels : 2 * levels])
    keep(0, masked(
        held[:, :, 2 * levels : depth] - 0.5 * (shift(u, -1) - shift(u, 1) + (south - north))
    ))
    side_slope[...] = (4.0 / 9.0) * (held[:, :, depth:] - 0.5)
    for k in range(ITERS - 1):
        here = side[k]
        north, south = beside_rows(here)
        twice = side_slope[...] * here - (4.0 / 9.0) * (shift(here, 1) + shift(here, -1) + (north + south))
        keep(k + 1, masked(0.5 * twice if k == 0 else twice - side[k - 1]))

    loads[2].wait()
    sums = []
    for k in range(ITERS):
        now = table[k]

        def following(e, count, stiff, inserted):
            here = now[pl.ds(e, count)]
            beside = shifted(here, neighbours) + inserted + (now[pl.ds(e - 1, count)] + now[pl.ds(e + 1, count)])
            twice = (4.0 / 9.0) * ((stiff - 0.5) * here - beside)
            if k == 0:
                return here, 0.5 * twice
            return here, twice - table[k - 1][pl.ds(e, count)]

        def step(i, carry):
            squares, cross = carry
            e = FIELDS + i * stride
            packed = past_ref[k, pl.ds(1 + i * (stride // FIELDS), stride // FIELDS)]
            here, value = following(e, stride, slope_ref[pl.ds(i * stride, stride)], insertions(packed, 0, stride))
            if k < ITERS - 1:
                table[k + 1][pl.ds(e, stride)] = value
            return squares + jnp.sum(here * here, axis=0), cross + jnp.sum(here * value, axis=0)

        zero = jnp.zeros((levels, points), F32)
        sums.append(lax.fori_loop(0, rows // stride, step, (zero, zero)))
        if k < ITERS - 1:
            reach = ITERS - 1 - k
            table[k + 1][first - reach : first] = top * following(
                first - reach, reach, above_ref[FIELDS - reach : FIELDS, depth:],
                insertions(past_ref[k, 0:1], FIELDS - reach, reach),
            )[1]
            table[k + 1][last + 1 : last + 1 + reach] = bottom * following(
                last + 1, reach, below_ref[0:reach, depth:], insertions(past_ref[k, groups + 1 :], 0, reach)
            )[1]

    lane = lanes((1, points))
    moments = jnp.zeros((1, points), F32)
    for i, value in enumerate([a for a, _ in sums] + [b for _, b in sums]):
        total = jnp.sum(jnp.sum(value, axis=0, keepdims=True), axis=1, keepdims=True)
        moments = jnp.where(lane == i, total, moments)
    moments_ref[...] = jnp.broadcast_to(moments, moments_ref.shape)


def make_basis(info, above, below, begun, sides, stiffness, ends, smooth, polar, devices):
    rows, levels, points = stiffness.shape
    depth = 3 * levels
    groups = rows // FIELDS + 2
    both = depth + levels
    vmem = pl.BlockSpec(memory_space=pltpu.VMEM)
    return pl.pallas_call(
        basis_kernel,
        in_specs=[pl.BlockSpec(memory_space=pltpu.SMEM)] + [pl.BlockSpec(memory_space=pl.ANY)] * 5 + [vmem] * 2,
        out_specs=(vmem,) * (ITERS + 3),
        out_shape=(pltpu.VMEM((rows + 2 * FIELDS, levels, points), F32),) * ITERS
        + (
            pltpu.VMEM((ITERS, groups, levels, points), F32),
            pltpu.HBM((polar, depth, points), F32),
            jax.ShapeDtypeStruct((devices, points), F32),
        ),
        scratch_shapes=[
            pltpu.VMEM((2, groups, both, points), F32),
            pltpu.VMEM(stiffness.shape, F32),
            pltpu.VMEM((polar + 2, depth, points), F32),
            pltpu.VMEM((polar // FIELDS, levels, points), F32),
            pltpu.VMEM((ITERS, 2, groups, levels, points), F32),
            pltpu.VMEM((2, groups, levels, points), F32),
            pltpu.VMEM(above.shape, F32),
            pltpu.VMEM(below.shape, F32),
            pltpu.SemaphoreType.DMA((5,)),
        ],
        cost_estimate=pl.CostEstimate(flops=40000000, bytes_accessed=24000000, transcendentals=0),
        compiler_params=params(16),
        name="basis",
    )(info, *[in_hbm(x) for x in (above, below, begun, sides, stiffness)], ends, smooth)


def solve(mu):
    gram = [[0.5 * (mu[i + j] + mu[abs(i - j)]) for j in range(ITERS + 1)] for i in range(ITERS)]

    def inner(a, b):
        return tree([x * tree([y * gram[i][j] for j, y in enumerate(b)]) for i, x in enumerate(a)])

    def image_of(a):
        out = [4.5 * x for x in a] + [jnp.zeros_like(a[0])]
        for k, x in enumerate(a):
            out[k + 1] = out[k + 1] + 2.25 * x
            out[abs(k - 1)] = out[abs(k - 1)] + 2.25 * x
        return out

    zero = jnp.zeros_like(mu[0])
    phi = []
    residual = [zero + 1.0]
    direction = residual
    norm = mu[0]
    for step in range(ITERS):
        image = image_of(direction)
        alpha = norm / inner(direction, image)
        phi = [x + alpha * y for x, y in zip(phi + [zero], direction)]
        if step < ITERS - 1:
            residual = [x - alpha * y for x, y in zip(residual + [zero], image)]
            following = inner(residual, residual)
            ratio = following / norm
            direction = [x + ratio * y for x, y in zip(residual, direction + [zero])]
            norm = following
    return phi


def finish_kernel(
    info_ref, spread_ref, filtered_hbm, caps_hbm, t0, t1, t2, t3, t4, past_ref, out_ref,
    coefficient_ref, filtered_ref, caps_ref, sems,
):
    table = [t0, t1, t2, t3, t4]
    _, levels, points = t0.shape
    block = out_ref.shape[0]
    g = pl.program_id(0)

    def fetch(i):
        part = pl.ds(i * block, block)
        return pltpu.make_async_copy(filtered_hbm.at[part], filtered_ref.at[part], sems.at[i])

    polar = caps_ref.shape[0]
    start, is_polar = info_ref[0], info_ref[1]
    fetch_caps = pltpu.make_async_copy(caps_hbm, caps_ref, sems.at[filtered_ref.shape[0] // block])

    @pl.when(g == 0)
    def _():
        fetch_caps.start()
        for i in range(filtered_ref.shape[0] // block):
            fetch(i).start()
        total = jnp.sum(spread_ref[...], axis=0, keepdims=True)
        lane = lanes(total.shape)
        picked = [
            jnp.sum(jnp.where(lane == i, total, 0.0), axis=1, keepdims=True) for i in range(2 * ITERS)
        ]
        mu = [picked[0], picked[ITERS]]
        for k in range(1, ITERS):
            mu += [2.0 * picked[k] - mu[0], 2.0 * picked[ITERS + k] - mu[1]]
        for k, value in enumerate(solve(mu)):
            coefficient_ref[k] = jnp.broadcast_to(value, (8, points))

    c = [jnp.concatenate([coefficient_ref[k]] * (levels // 8), axis=0) for k in range(ITERS)]

    fetch(g).wait()

    @pl.when(g == 0)
    def _():
        fetch_caps.wait()

    @pl.when((is_polar == 1) & (g == start // block))
    def _():
        filtered_ref[pl.ds(start, polar)] = caps_ref[...]

    def phi_of(e):
        return tree([c[k] * table[k][e] for k in range(ITERS)])

    lane = lanes((levels, points))
    stride = FIELDS

    def step(i, carry):
        first = i * stride
        row = g * block + first
        near = list(carry) + [phi_of(FIELDS + row + 1 + j) for j in range(stride)]
        packed = tree([c[k] * past_ref[k, 1 + row // FIELDS] for k in range(ITERS)])
        old = [filtered_ref[row + j] for j in range(stride)]
        new = []
        for j in range(stride):
            here = near[j + 1]
            inserted = unpack_lanes(packed, j)
            east = jnp.where(lane == points - 1, inserted, shift(here, -1))
            west = jnp.where(lane == 0, inserted, shift(here, 1))
            new.append(old[j][0:levels] - 0.5 * (east - west))
            new.append(old[j][levels : 2 * levels] - 0.5 * (near[j + 2] - near[j]))
            new.append(old[j][2 * levels :] - here)
        for j in range(stride):
            for part in range(3):
                out_ref[first + j, part * levels : (part + 1) * levels] = new[3 * j + part]
        return near[stride], near[stride + 1]

    e = FIELDS + g * block
    lax.fori_loop(0, block // stride, step, (phi_of(e - 1), phi_of(e)), unroll=True)


def finish(info, spread, filtered, caps, table):
    rows, depth, points = filtered.shape
    block = 32
    vmem = pl.BlockSpec(memory_space=pltpu.VMEM)
    piece = pl.BlockSpec((block, depth, points), lambda g: (g, 0, 0))
    return pl.pallas_call(
        finish_kernel,
        grid=(rows // block,),
        in_specs=[pl.BlockSpec(memory_space=pltpu.SMEM), vmem] + [pl.BlockSpec(memory_space=pl.ANY)] * 2 + [vmem] * (ITERS + 1),
        out_specs=piece,
        out_shape=jax.ShapeDtypeStruct((rows, depth, points), F32),
        scratch_shapes=[
            pltpu.VMEM((ITERS, 8, points), F32),
            pltpu.VMEM((rows, depth, points), F32),
            pltpu.VMEM(caps.shape, F32),
            pltpu.SemaphoreType.DMA((rows // block + 1,)),
        ],
        cost_estimate=pl.CostEstimate(flops=20000000, bytes_accessed=17000000, transcendentals=0),
        compiler_params=params(12),
        name="finish",
    )(info, spread, in_hbm(filtered), in_hbm(caps), *table)


def shards(state, weights, owners, source_rows, cutoffs, stiffness):
    rows, comps, levels, points = state.shape
    depth = comps * levels
    n_lon = lax.axis_size("lon")
    n_lat = lax.axis_size("lat")
    devices = n_lon * n_lat
    band = lax.axis_index("lat")
    north, south = band == 0, band == n_lat - 1
    polar = cutoffs.shape[0] // 2
    line = lax.axis_index("lon") * polar // n_lon
    info = jnp.stack(
        [
            jnp.where(north, 0, rows - polar),
            (north | south).astype(jnp.int32),
            (band > 0).astype(jnp.int32),
            (band < n_lat - 1).astype(jnp.int32),
            cutoffs[jnp.where(north, line, polar + line)],
        ]
    ).astype(jnp.int32)

    requests, place = make_requests(owners[:, :, 0], source_rows)
    asked = exchange(requests, BOTH)[:, :2]
    asked, ahead, ahead_weights = lax.optimization_barrier((asked, stiffness, weights))
    moved = exchange(state[asked], BOTH).reshape(2 * devices, depth, points)
    moved, rim_weights, *stiff = lax.optimization_barrier(
        (moved, edge_weights(ahead_weights)) + tuple(pack_stiffness(ahead))
    )

    place = place[0]
    caps, last, first = make_caps(place, info, moved, weights, stiffness, polar)
    lines = exchange(caps.reshape(n_lon, -1, points), "lon")
    place, caps = lax.optimization_barrier((place, caps))
    to_east, to_west, own = make_edges(place, moved, rim_weights, stiff)
    west, east = from_sides(to_east, to_west)
    passed = low_pass(info, lines)
    smooth = exchange(passed, "lon")
    _, west_late, east_late = lax.optimization_barrier((passed, west, east))
    above, below = from_ends(*make_ends(last, first, west_late, east_late))
    arrived, begun, sides, near = prepare(place, info, moved, weights, west, east, own)
    *table, caps, moments = make_basis(info, above, below, begun, sides, stiffness, near, smooth, polar, devices)
    out = finish(info, exchange(moments, BOTH), arrived, caps, table)
    return out.reshape(rows, comps, levels, points)


def solution(mesh):
    in_specs = (
        P("lat", None, None, "lon"),
        P("lat", None, "lon"),
        P("lon", "lat", None),
        P("lon", "lat"),
        P(),
        P("lat", None, "lon"),
    )
    out_specs = P("lat", None, None, "lon")
    return jax.shard_map(shards, mesh=mesh, in_specs=in_specs, out_specs=out_specs, check_vma=False)
```

```python
import functools

import numpy as np
import jax
import jax.numpy as jnp
from jax import lax
from jax.experimental import pallas as pl
from jax.experimental.pallas import tpu as pltpu
from jax.sharding import PartitionSpec as P

ITERS = 5
BOTH = ("lon", "lat")
HIGHEST = lax.Precision.HIGHEST
FIELD = 16
FIELDS = 8
F32 = jnp.float32
MIB = 1024 * 1024


def params(mib):
    return pltpu.CompilerParams(vmem_limit_bytes=mib * MIB)


def in_hbm(x):
    return pltpu.with_memory_space_constraint(x, pltpu.HBM)


def exchange(block, axes):
    return lax.all_to_all(block, axes, split_axis=0, concat_axis=0, tiled=True)


def lanes(shape):
    return lax.broadcasted_iota(jnp.int32, shape, len(shape) - 1)


def pack_lanes(shape, rows):
    field = lanes(shape) // FIELD
    packed = jnp.zeros(shape, F32)
    for f, row in enumerate(rows):
        packed = jnp.where(field == f, pltpu.roll(row, (FIELD * f + 8) % 128, len(shape) - 1), packed)
    return packed


def unpack_lanes(packed, f):
    return pltpu.roll(packed, (-(FIELD * f + 8)) % 128, packed.ndim - 1)


def request_kernel(row_ref, wanted_ref, request_ref, place_ref):
    row = row_ref[...]
    size = row.shape[1]
    down = lax.broadcasted_iota(jnp.int32, (size, size), 0)
    across = lax.broadcasted_iota(jnp.int32, (size, size), 1)
    owner = jnp.broadcast_to(row, (size, size))
    earlier = (owner.T == owner) & (down < across)
    slot = jnp.sum(jnp.where(earlier, 1.0, 0.0), axis=0, keepdims=True)
    wanted = wanted_ref[...].astype(F32)
    out = jnp.zeros((size, size), F32)
    for s in range(2):
        hit = jnp.where((owner == down) & (slot == s), wanted, 0.0)
        out = jnp.where(across == s, jnp.sum(hit, axis=1, keepdims=True), out)
    request_ref[...] = out.astype(jnp.int32)
    place_ref[...] = 2 * row + slot.astype(jnp.int32)


def make_requests(owner, wanted):
    rows = wanted.shape[1]
    return pl.pallas_call(
        request_kernel,
        out_shape=(
            jax.ShapeDtypeStruct((rows, rows), jnp.int32),
            jax.ShapeDtypeStruct((1, rows), jnp.int32),
        ),
        cost_estimate=pl.CostEstimate(flops=200000, bytes_accessed=200000, transcendentals=0),
        compiler_params=params(2),
        name="requests",
    )(in_hbm(owner), in_hbm(wanted))


def ways(axis, wrap):
    count = lax.axis_size(axis)
    up = [(i, (i + 1) % count) for i in range(count if wrap else count - 1)]
    return up, [(b, a) for a, b in up]


def from_sides(to_east, to_west):
    east, west = ways("lon", True)
    return lax.ppermute(to_east, "lon", east), lax.ppermute(to_west, "lon", west)


def from_ends(last, first):
    north, south = ways("lat", False)
    return lax.ppermute(last, "lat", north), lax.ppermute(first, "lat", south)


def low_half(x):
    return lanes(x.shape) % FIELD < FIELD // 2


def shift(x, by):
    return pltpu.roll(x, by % 128, x.ndim - 1)


def for_sides(even, odd):
    low = low_half(even)
    return jnp.where(low, even, shift(odd, 8)), jnp.where(low, shift(even, -8), odd)


def strips(from_west, from_east, own, parity):
    low = low_half(own)
    if parity == 0:
        return jnp.where(low, from_west, own), jnp.where(low, own, shift(from_east, 8))
    return jnp.where(low, shift(from_west, -8), own), jnp.where(low, own, from_east)


def beyond(left, right):
    return jnp.where(lanes(left.shape) % FIELD == FIELD // 2, shift(left, 1), shift(right, -1))


def insertion(packed, f):
    lane = lanes(packed.shape)
    return jnp.where((lane == 0) | (lane == 127), unpack_lanes(packed, f), 0.0)


def insertions(packed, first, count):
    return jnp.stack([insertion(packed[(first + i) // FIELDS], (first + i) % FIELDS) for i in range(count)])


def caps_kernel(
    place_ref, info_ref, moved_hbm, weights_hbm, stiffness_hbm, caps_ref, last_ref, first_ref,
    held, weights_ref, stiffness_ref, row_sems, sems,
):
    polar = caps_ref.shape[0]
    depth = caps_ref.shape[1]
    rows = weights_hbm.shape[0]
    start = info_ref[0]
    spans = [(start, 0, polar), (0, polar, FIELDS), (rows - FIELDS, polar + FIELDS, FIELDS)]
    copies = []
    for n, (row, at, count) in enumerate(spans):
        copies.append(
            pltpu.make_async_copy(weights_hbm.at[pl.ds(row, count)], weights_ref.at[pl.ds(at, count)], sems.at[n])
        )
        copies += [
            pltpu.make_async_copy(moved_hbm.at[place_ref[row + i]], held.at[at + i], row_sems.at[at + i])
            for i in range(count)
        ]
    for end, row in enumerate((0, rows - FIELDS)):
        copies.append(
            pltpu.make_async_copy(stiffness_hbm.at[pl.ds(row, FIELDS)], stiffness_ref.at[end], sems.at[3 + end])
        )
    for copy in copies:
        copy.start()
    for copy in copies:
        copy.wait()
    values = [
        jnp.dot(held[i], weights_ref[i], preferred_element_type=F32) for i in range(polar + 2 * FIELDS)
    ]
    for i in range(polar):
        caps_ref[i] = values[i]
    for end, ref in enumerate((first_ref, last_ref)):
        low = polar + end * FIELDS
        rim = values[low : low + FIELDS]
        stiff = [stiffness_ref[end, f] for f in range(FIELDS)]
        for f in range(FIELDS):
            ref[f, 0:depth] = rim[f]
            ref[f, depth:] = stiff[f]
        ref[FIELDS, 0:depth] = pack_lanes(rim[0].shape, rim)
        ref[FIELDS, depth:] = pack_lanes(stiff[0].shape, stiff)


def make_caps(place, info, moved, weights, stiffness, polar):
    _, depth, points = moved.shape
    levels = stiffness.shape[1]
    smem = pl.BlockSpec(memory_space=pltpu.SMEM)
    hbm = pl.BlockSpec(memory_space=pl.ANY)
    count = polar + 2 * FIELDS
    rim = jax.ShapeDtypeStruct((FIELDS + 1, depth + levels, points), F32)
    return pl.pallas_call(
        caps_kernel,
        in_specs=[smem, smem, hbm, hbm, hbm],
        out_specs=[pl.BlockSpec(memory_space=pltpu.VMEM)] * 3,
        out_shape=(jax.ShapeDtypeStruct((polar, depth, points), F32), rim, rim),
        scratch_shapes=[
            pltpu.VMEM((count, depth, points), moved.dtype),
            pltpu.VMEM((count, points, points), weights.dtype),
            pltpu.VMEM((2, FIELDS, levels, points), F32),
            pltpu.SemaphoreType.DMA((count,)),
            pltpu.SemaphoreType.DMA((5,)),
        ],
        cost_estimate=pl.CostEstimate(flops=60000000, bytes_accessed=2400000, transcendentals=0),
        compiler_params=params(6),
        name="caps",
    )(place, info, in_hbm(moved), in_hbm(weights), in_hbm(stiffness))


def stiff_kernel(stiffness_ref, east_ref, west_ref, own_ref):
    def pair(g, carry):
        packed = []
        for h in range(2):
            rows = [stiffness_ref[(2 * g + h) * FIELDS + f] for f in range(FIELDS)]
            packed.append(pack_lanes(rows[0].shape, rows))
        east_ref[g], west_ref[g] = for_sides(*packed)
        own_ref[2 * g], own_ref[2 * g + 1] = packed
        return carry

    lax.fori_loop(0, east_ref.shape[0], pair, 0)


def pack_stiffness(stiffness):
    rows, levels, points = stiffness.shape
    side = pltpu.HBM((rows // (2 * FIELDS), levels, points), F32)
    return pl.pallas_call(
        stiff_kernel,
        out_shape=(side, side, pltpu.HBM((rows // FIELDS, levels, points), F32)),
        cost_estimate=pl.CostEstimate(flops=1000000, bytes_accessed=1300000, transcendentals=0),
        compiler_params=params(4),
        name="pack_stiffness",
    )(in_hbm(stiffness))


def edge_weights_kernel(weights_ref, out_ref):
    rows = [weights_ref[f].astype(F32) for f in range(FIELDS)]
    out_ref[0] = pack_lanes(rows[0].shape, rows).astype(out_ref.dtype)


def edge_weights(weights):
    rows, points, _ = weights.shape
    return pl.pallas_call(
        edge_weights_kernel,
        grid=(rows // FIELDS,),
        in_specs=[pl.BlockSpec((FIELDS, points, points), lambda g: (g, 0, 0))],
        out_specs=pl.BlockSpec((1, points, points), lambda g: (g, 0, 0)),
        out_shape=pltpu.HBM((rows // FIELDS, points, points), weights.dtype),
        cost_estimate=pl.CostEstimate(flops=2000000, bytes_accessed=5000000, transcendentals=0),
        compiler_params=params(6),
        name="edge_weights",
    )(in_hbm(weights))


def edges_kernel(
    place_ref, moved_hbm, east_hbm, west_hbm, own_hbm, weights_hbm, east_ref, west_ref, own_ref,
    moved_ref, weights_ref, sems,
):
    depth = moved_ref.shape[1]
    levels = own_hbm.shape[1]
    loads = [
        pltpu.make_async_copy(moved_hbm, moved_ref, sems.at[0]),
        pltpu.make_async_copy(weights_hbm, weights_ref, sems.at[1]),
        pltpu.make_async_copy(east_hbm, east_ref.at[:, pl.ds(depth, levels)], sems.at[2]),
        pltpu.make_async_copy(west_hbm, west_ref.at[:, pl.ds(depth, levels)], sems.at[3]),
        pltpu.make_async_copy(own_hbm, own_ref.at[:, pl.ds(depth, levels)], sems.at[4]),
    ]
    for load in loads:
        load.start()
    for load in loads[:2]:
        load.wait()
    shape = (depth, moved_ref.shape[2])
    field = lanes(shape) // FIELD

    def pair(g, carry):
        packed = []
        for h in range(2):
            group = 2 * g + h
            sources = [moved_ref[place_ref[group * FIELDS + f]] for f in range(FIELDS)]
            product = jnp.dot(
                jnp.concatenate(sources, axis=0), weights_ref[group], preferred_element_type=F32
            )
            value = jnp.zeros(shape, F32)
            for f in range(FIELDS):
                value = jnp.where(field == f, product[f * depth : (f + 1) * depth], value)
            packed.append(value)
        east, west = for_sides(*packed)
        east_ref[g, 0:depth] = east
        west_ref[g, 0:depth] = west
        for h in range(2):
            own_ref[2 * g + h, 0:depth] = packed[h]
        return carry

    lax.fori_loop(0, east_ref.shape[0], pair, 0, unroll=True)
    for load in loads[2:]:
        load.wait()


def make_edges(place, moved, weights, stiff):
    _, depth, points = moved.shape
    groups, levels, _ = stiff[2].shape
    both = depth + levels
    vmem = pl.BlockSpec(memory_space=pltpu.VMEM)
    hbm = pl.BlockSpec(memory_space=pl.ANY)
    side = jax.ShapeDtypeStruct((groups // 2, both, points), F32)
    return pl.pallas_call(
        edges_kernel,
        in_specs=[pl.BlockSpec(memory_space=pltpu.SMEM)] + [hbm] * 5,
        out_specs=[vmem] * 3,
        out_shape=(side, side, pltpu.HBM((groups, both, points), F32)),
        scratch_shapes=[
            pltpu.VMEM(moved.shape, moved.dtype),
            pltpu.VMEM(weights.shape, weights.dtype),
            pltpu.SemaphoreType.DMA((5,)),
        ],
        cost_estimate=pl.CostEstimate(flops=10000000000, bytes_accessed=5000000, transcendentals=0),
        compiler_params=params(10),
        name="edges",
    )(place, in_hbm(moved), *[in_hbm(x) for x in stiff], in_hbm(weights))


def ends_kernel(last_rim_ref, first_rim_ref, west_ref, east_ref, last_ref, first_ref):
    pairs = west_ref.shape[0]
    for rim, ref, end, pair in ((first_rim_ref, first_ref, 0, 0), (last_rim_ref, last_ref, 1, pairs - 1)):
        ref[0:FIELDS] = rim[0:FIELDS]
        ref[FIELDS], ref[FIELDS + 1] = strips(west_ref[pair], east_ref[pair], rim[FIELDS], end)


def make_ends(last, first, west, east):
    _, both, points = last.shape
    shape = jax.ShapeDtypeStruct((FIELDS + 2, both, points), F32)
    return pl.pallas_call(
        ends_kernel,
        out_shape=(shape, shape),
        cost_estimate=pl.CostEstimate(flops=100000, bytes_accessed=2000000, transcendentals=0),
        compiler_params=params(6),
        name="ends",
    )(last, first, west, east)


def tree(terms):
    while len(terms) > 1:
        terms = [a + b for a, b in zip(terms[::2], terms[1::2])] + terms[len(terms) // 2 * 2 :]
    return terms[0]


def halves(table):
    high = table.astype(jnp.bfloat16)
    return np.stack([high, (table - high.astype(np.float64)).astype(jnp.bfloat16)])


def filter_tables(parts, points):
    total = parts * points
    half = parts // 2 + 1
    k1, p = np.arange(half), np.arange(points)
    twist = 2 * np.pi * np.outer(k1, p) / total
    inner = 2 * np.pi * np.outer(p, p) / points
    c, s = np.cos(inner), np.sin(inner)
    forward = np.block([[c, -s], [s, c]])
    inverse = np.block([[c, s], [-s, c]])
    twist = np.concatenate([np.cos(twist), np.sin(twist)]).astype(np.float32)
    return twist, halves(forward), halves(inverse)


def cosine_sums(v, parts):
    mid, quarter = parts // 2, parts // 4
    plus = [v[j - 1] + v[mid - j - 1] for j in range(1, quarter)]
    minus = [v[j - 1] - v[mid - j - 1] for j in range(1, quarter)]
    out = []
    for m in range(mid + 1):
        folded = plus if m % 2 == 0 else minus
        terms = [float(np.cos(2 * np.pi * m * j / parts)) * folded[j - 1] for j in range(1, quarter)]
        if m % 2 == 0:
            terms.append(v[quarter - 1] if m % 4 == 0 else -v[quarter - 1])
        out.append(tree(terms))
    return out


def sine_sums(v, parts):
    mid, quarter = parts // 2, parts // 4
    plus = [v[j - 1] + v[mid - j - 1] for j in range(1, quarter)]
    minus = [v[j - 1] - v[mid - j - 1] for j in range(1, quarter)]
    out = []
    for m in range(1, mid):
        folded = minus if m % 2 == 0 else plus
        terms = [float(np.sin(2 * np.pi * m * j / parts)) * folded[j - 1] for j in range(1, quarter)]
        if m % 2 == 1:
            terms.append(v[quarter - 1] if m % 4 == 1 else -v[quarter - 1])
        out.append(tree(terms))
    return out


def product(x, table_ref):
    high, low = split(x)
    count = x.shape[0]
    both = jnp.dot(jnp.concatenate([high, low], axis=0), table_ref[0], preferred_element_type=F32)
    return both[:count] + both[count:] + jnp.dot(high, table_ref[1], preferred_element_type=F32)


def filter_kernel(
    info_ref, lines_ref, twist_hbm, forward_hbm, inverse_hbm, out_ref,
    work, back, twist_ref, forward_ref, inverse_ref, sems,
):
    parts, count, points = lines_ref.shape
    pairs = [(twist_hbm, twist_ref), (forward_hbm, forward_ref), (inverse_hbm, inverse_ref)]
    loads = [pltpu.make_async_copy(a, b, sems.at[i]) for i, (a, b) in enumerate(pairs)]
    for load in loads:
        load.start()
    total = parts * points
    mid = parts // 2
    cutoff = info_ref[4]
    tiles = count // 8
    loads[0].wait()
    for t in range(tiles):
        x = [lines_ref[d, 8 * t : 8 * t + 8, :] for d in range(parts)]
        even = cosine_sums([x[d] + x[parts - d] for d in range(1, mid)], parts)
        odd = sine_sums([x[d] - x[parts - d] for d in range(1, mid)], parts)
        ends = (x[0] + x[mid], x[0] - x[mid])
        for k in range(mid + 1):
            real = ends[k % 2] + even[k]
            row = k * count + 8 * t
            tc, ts = twist_ref[k : k + 1, :], twist_ref[mid + 1 + k : mid + 2 + k, :]
            if k in (0, mid):
                work[row : row + 8, 0:points] = real * tc
                work[row : row + 8, points:] = -real * ts
            else:
                imag = odd[k - 1]
                work[row : row + 8, 0:points] = real * tc - imag * ts
                work[row : row + 8, points:] = -imag * tc - real * ts
    loads[1].wait()
    spectrum = product(work[...], forward_ref)
    shape = spectrum.shape
    wave = lax.broadcasted_iota(jnp.int32, shape, 0) // count + parts * (lanes(shape) % points)
    kept = (wave <= cutoff) | (wave >= total - cutoff)
    spectrum = jnp.where(kept, spectrum * (1.0 / total), 0.0)
    loads[2].wait()
    back[...] = product(spectrum, inverse_ref)
    for t in range(tiles):
        real, imag = [], []
        for k in range(mid + 1):
            row = k * count + 8 * t
            br, bi = back[row : row + 8, 0:points], back[row : row + 8, points:]
            tc, ts = twist_ref[k : k + 1, :], twist_ref[mid + 1 + k : mid + 2 + k, :]
            real.append(br * tc - bi * ts)
            if k not in (0, mid):
                imag.append(br * ts + bi * tc)
        even = cosine_sums(real[1:mid], parts)
        odd = sine_sums(imag, parts)
        ends = (real[0] + real[mid], real[0] - real[mid])
        for d in range(mid + 1):
            value = ends[d % 2] + 2.0 * even[d]
            if d in (0, mid):
                out_ref[d, 8 * t : 8 * t + 8, :] = value
            else:
                out_ref[d, 8 * t : 8 * t + 8, :] = value - 2.0 * odd[d - 1]
                out_ref[parts - d, 8 * t : 8 * t + 8, :] = value + 2.0 * odd[d - 1]
    shape = (8, points)
    low = lanes(shape) < points // 2
    for d in range(parts):
        rows = [
            jnp.where(
                low,
                out_ref[(d + 1) % parts, 8 * t : 8 * t + 8, :],
                out_ref[(d - 1) % parts, 8 * t : 8 * t + 8, :],
            )
            for t in range(tiles)
        ]
        out_ref[d, count : count + 8, :] = pack_lanes(shape, rows)


def low_pass(info, lines):
    parts, count, points = lines.shape
    tables = filter_tables(parts, points)
    rows = (parts // 2 + 1) * count
    vmem = pl.BlockSpec(memory_space=pltpu.VMEM)
    return pl.pallas_call(
        filter_kernel,
        in_specs=[pl.BlockSpec(memory_space=pltpu.SMEM)] + [vmem] + [pl.BlockSpec(memory_space=pl.ANY)] * 3,
        out_specs=vmem,
        out_shape=pltpu.HBM((parts, count + 8, points), F32),
        scratch_shapes=[pltpu.VMEM((rows, 2 * points), F32)] * 2
        + [pltpu.VMEM(x.shape, x.dtype) for x in tables]
        + [pltpu.SemaphoreType.DMA((3,))],
        cost_estimate=pl.CostEstimate(flops=700000000, bytes_accessed=1400000, transcendentals=0),
        compiler_params=params(8),
        name="low_pass",
    )(info, lines, *[in_hbm(jnp.asarray(x)) for x in tables])


def split(x):
    high = x.astype(jnp.bfloat16)
    return high, (x - high.astype(F32)).astype(jnp.bfloat16)


def shift_matrix(points, left, right):
    source = lax.broadcasted_iota(jnp.int32, (2 * points, points), 0) % points
    target = lax.broadcasted_iota(jnp.int32, (2 * points, points), 1)
    west, east = source + 1 == target, source == target + 1
    return (jnp.where(west, left, 0.0) + jnp.where(east, right, 0.0)).astype(jnp.bfloat16)


def shifted(x, matrix):
    flat = x.reshape(-1, x.shape[-1])
    out = jnp.dot(jnp.concatenate(split(flat), axis=1), matrix, preferred_element_type=F32)
    return out.reshape(x.shape)


def prepare_kernel(
    place_ref, info_ref, moved_hbm, weights_hbm, west_hbm, east_hbm, own_hbm,
    arrived_hbm, begun_hbm, strips_ref, ends_ref,
    moved_ref, weights_ref, begun_ref, wide, past, west_ref, east_ref, own_ref, sems, weight_sems, row_sems, save_sems,
):
    rows, levels, points = begun_ref.shape
    depth = wide.shape[1]
    polar = 16
    pieces, stride = rows // polar, 2 * polar
    start, is_polar = info_ref[0], info_ref[1]
    pairs = [(west_hbm, west_ref), (east_hbm, east_ref), (own_hbm, own_ref), (moved_hbm, moved_ref)]
    loads = [pltpu.make_async_copy(a, b, sems.at[i]) for i, (a, b) in enumerate(pairs)]

    def fetch(i):
        piece = pl.ds(i * polar, polar)
        return pltpu.make_async_copy(weights_hbm.at[piece], weights_ref.at[piece], weight_sems.at[i])

    def save_rows(i):
        return pltpu.make_async_copy(
            wide.at[pl.ds(1 + i * polar, polar)], arrived_hbm.at[pl.ds(i * polar, polar)], row_sems.at[i]
        )

    def save(i):
        piece = pl.ds(i * stride, stride)
        return pltpu.make_async_copy(begun_ref.at[piece], begun_hbm.at[piece], save_sems.at[i])

    for load in loads:
        load.start()
    for i in range(pieces):
        fetch(i).start()
    zero = jnp.zeros((1, depth, points), F32)
    for row in (0, rows + 1):
        wide[row : row + 1] = zero
    for load in loads[:3]:
        load.wait()
    for g in range(rows // FIELDS):
        left, right = strips(west_ref[g // 2], east_ref[g // 2], own_ref[g], g % 2)
        strips_ref[0, g], strips_ref[1, g] = left, right
        past[g] = beyond(left[0:levels], right[0:levels])

    @pl.when(is_polar == 1)
    def _():
        past[pl.ds(start // FIELDS, polar // FIELDS)] = jnp.zeros((polar // FIELDS, levels, points), F32)

    loads[3].wait()
    difference = shift_matrix(points, -0.5, 0.5)
    half_sign = jnp.where(lanes((1, 1, points)) == 0, 0.5, -0.5)

    def interpolate(i):
        fetch(i).wait()
        first = i * polar
        sources = [moved_ref[place_ref[first + j]] for j in range(polar)]
        values = [
            jnp.dot(source, weights_ref[first + j], preferred_element_type=F32) for j, source in enumerate(sources)
        ]
        for j, value in enumerate(values):
            wide[1 + first + j] = value

        @pl.when((is_polar == 1) & (start // polar == i))
        def _():
            wide[1 + first : 1 + first + polar] = jnp.zeros((polar, depth, points), F32)

        save_rows(i).start()

    def step(i):
        e = 1 + i * stride
        part = lambda e, which: wide[pl.ds(e, stride), which * levels : (which + 1) * levels]
        groups = past[pl.ds(i * (stride // FIELDS), stride // FIELDS)]
        across = shifted(part(e, 0), difference) - half_sign * insertions(groups, 0, stride)
        begun_ref[pl.ds(i * stride, stride)] = part(e, 2) - (across + 0.5 * (part(e + 1, 1) - part(e - 1, 1)))
        save(i).start()

    for i in range(pieces):
        interpolate(i)
        if i % 2 == 0 and i > 0:
            step(i // 2 - 1)
    step(pieces // 2 - 1)
    ends_ref[0] = wide[1, levels : 2 * levels]
    ends_ref[1] = wide[rows, levels : 2 * levels]
    for i in range(pieces):
        save_rows(i).wait()
    for i in range(rows // stride):
        save(i).wait()


def prepare(place, info, moved, weights, west, east, own):
    rows, points, _ = weights.shape
    groups, both, _ = own.shape
    depth = moved.shape[1]
    levels = both - depth
    vmem = pl.BlockSpec(memory_space=pltpu.VMEM)
    hbm = pl.BlockSpec(memory_space=pl.ANY)
    return pl.pallas_call(
        prepare_kernel,
        in_specs=[pl.BlockSpec(memory_space=pltpu.SMEM)] * 2 + [hbm] * 5,
        out_specs=[hbm, hbm, vmem, vmem],
        out_shape=(
            pltpu.HBM((rows, depth, points), F32),
            pltpu.HBM((rows, levels, points), F32),
            pltpu.HBM((2, groups, both, points), F32),
            jax.ShapeDtypeStruct((2, levels, points), F32),
        ),
        scratch_shapes=[
            pltpu.VMEM(moved.shape, moved.dtype),
            pltpu.VMEM(weights.shape, weights.dtype),
            pltpu.VMEM((rows, levels, points), F32),
            pltpu.VMEM((rows + 2, depth, points), F32),
            pltpu.VMEM((groups, levels, points), F32),
            pltpu.VMEM(west.shape, F32),
            pltpu.VMEM(east.shape, F32),
            pltpu.VMEM(own.shape, F32),
            pltpu.SemaphoreType.DMA((4,)),
            pltpu.SemaphoreType.DMA((rows // 16,)),
            pltpu.SemaphoreType.DMA((rows // 16,)),
            pltpu.SemaphoreType.DMA((rows // 32,)),
        ],
        cost_estimate=pl.CostEstimate(flops=20000000000, bytes_accessed=16000000, transcendentals=0),
        compiler_params=params(22),
        name="prepare",
    )(place, info, *[in_hbm(x) for x in (moved, weights, west, east, own)])


def basis_kernel(
    info_ref, above_hbm, below_hbm, begun_hbm, strips_hbm, stiffness_hbm, ends_ref, smooth_ref,
    t0, t1, t2, t3, t4, past_ref, caps_ref, moments_ref,
    held, slope_ref, wide, polar_strips, side, side_slope, above_ref, below_ref, sems,
):
    rows, levels, points = slope_ref.shape
    depth = 3 * levels
    polar = caps_ref.shape[0]
    groups = rows // FIELDS
    table = [t0, t1, t2, t3, t4]
    start, is_polar = info_ref[0], info_ref[1]
    top, bottom = info_ref[2].astype(F32), info_ref[3].astype(F32)
    stride = 128
    first, last = FIELDS, FIELDS + rows - 1
    loads = [
        pltpu.make_async_copy(strips_hbm, held.at[:, pl.ds(1, groups)], sems.at[0]),
        pltpu.make_async_copy(begun_hbm, t0.at[pl.ds(first, rows)], sems.at[1]),
        pltpu.make_async_copy(stiffness_hbm, slope_ref, sems.at[2]),
    ]
    halo = [
        pltpu.make_async_copy(above_hbm, above_ref, sems.at[3]),
        pltpu.make_async_copy(below_hbm, below_ref, sems.at[4]),
    ]
    for load in halo + loads:
        load.start()
    difference = shift_matrix(points, -0.5, 0.5)
    neighbours = shift_matrix(points, 1.0, 1.0)
    half_sign = jnp.where(lanes((1, 1, points)) == 0, 0.5, -0.5)

    def component(x, which):
        return x[..., which * levels : (which + 1) * levels, :]

    def rhs(u, theta, north, south, inserted):
        return theta - (shifted(u, difference) - half_sign * inserted + 0.5 * (south - north))

    for load in halo:
        load.wait()
    nearest = []
    for end, ref in enumerate((above_ref, below_ref)):
        group = 0 if end == 0 else groups + 1
        left, right = ref[FIELDS], ref[FIELDS + 1]
        held[0, group], held[1, group] = left, right
        packed = beyond(left[0:levels], right[0:levels])[None]
        fields = ref[0:FIELDS, 0:depth]
        v = component(fields, 1)
        low, count = (FIELDS - ITERS, ITERS) if end == 0 else (0, ITERS)
        if end == 0:
            north = v[low - 1 : FIELDS - 1]
            south = jnp.concatenate([v[low + 1 :], ends_ref[0:1]], axis=0)
            nearest.append(0.5 * v[FIELDS - 1 :])
        else:
            north = jnp.concatenate([ends_ref[1:2], v[0 : count - 1]], axis=0)
            south = v[1 : count + 1]
            nearest.append(0.5 * v[0:1])
        value = rhs(
            component(fields, 0)[low : low + count], component(fields, 2)[low : low + count], north, south,
            insertions(packed, low, count),
        )
        place = first - FIELDS + low if end == 0 else last + 1
        t0[place : place + count] = (top if end == 0 else bottom) * value
    loads[0].wait()
    loads[1].wait()
    t0[first : first + 1] = t0[first : first + 1] + nearest[0]
    t0[last : last + 1] = t0[last : last + 1] - nearest[1]

    @pl.when(is_polar == 1)
    def _():
        half = depth // 2
        zero = jnp.zeros((1, depth, points), F32)
        wide[0:1] = zero
        wide[polar + 1 :] = zero
        shape = (depth, points)
        field = lanes(shape) // FIELD
        low = low_half(jnp.zeros(shape, F32))
        for group in range(polar // FIELDS):
            own, outer = jnp.zeros(shape, F32), jnp.zeros(shape, F32)
            for f in range(FIELDS):
                i = group * FIELDS + f
                lines = [smooth_ref[2 * i], smooth_ref[2 * i + 1]]
                row = jnp.concatenate([line[0:half] for line in lines], axis=0)
                caps_ref[i] = row
                wide[1 + i] = row
                edges = [shift(line[half:], FIELD * (f - t)) for line in lines for t in range(half // 8)]
                own = jnp.where(field == f, shift(row, FIELD * f + 8), own)
                outer = jnp.where(field == f, jnp.concatenate(edges, axis=0), outer)
            left, right = jnp.where(low, outer, own), jnp.where(low, own, outer)
            place = 1 + start // FIELDS + group
            held[0, place, 0:depth] = left
            held[1, place, 0:depth] = right
            polar_strips[group] = beyond(left[0:levels], right[0:levels])
        u, v, theta = [component(wide[...], which) for which in range(3)]
        here = pl.ds(first + start, polar)
        t0[here] = t0[here] + rhs(
            u[1:-1], theta[1:-1], v[:-2], v[2:], insertions(polar_strips[...], 0, polar)
        )

        @pl.when(start == 0)
        def _():
            e = first + polar
            t0[e : e + 1] = t0[e : e + 1] + 0.5 * v[polar : polar + 1]

        @pl.when(start != 0)
        def _():
            e = last - polar
            t0[e : e + 1] = t0[e : e + 1] - 0.5 * v[1:2]

    def beside_rows(x):
        lane = lanes(x.shape)
        down, up = shift(x, FIELD), shift(x, -FIELD)
        before = jnp.concatenate([down[:, :1], down[:, :-1]], axis=1)
        after = jnp.concatenate([up[:, 1:], up[:, -1:]], axis=1)
        return jnp.where(lane < FIELD, before, down), jnp.where(lane >= 128 - FIELD, after, up)

    def masked(x):
        return jnp.concatenate([top * x[:, :1], x[:, 1:-1], bottom * x[:, -1:]], axis=1)

    def keep(k, x):
        side[k] = x
        past_ref[k] = beyond(x[0], x[1])

    u = held[:, :, 0:levels]
    north, south = beside_rows(held[:, :, levels : 2 * levels])
    keep(0, masked(
        held[:, :, 2 * levels : depth] - 0.5 * (shift(u, -1) - shift(u, 1) + (south - north))
    ))
    side_slope[...] = (4.0 / 9.0) * (held[:, :, depth:] - 0.5)
    for k in range(ITERS - 1):
        here = side[k]
        north, south = beside_rows(here)
        twice = side_slope[...] * here - (4.0 / 9.0) * (shift(here, 1) + shift(here, -1) + (north + south))
        keep(k + 1, masked(0.5 * twice if k == 0 else twice - side[k - 1]))

    loads[2].wait()
    sums = []
    for k in range(ITERS):
        now = table[k]

        def following(e, count, stiff, inserted):
            here = now[pl.ds(e, count)]
            beside = shifted(here, neighbours) + inserted + (now[pl.ds(e - 1, count)] + now[pl.ds(e + 1, count)])
            twice = (4.0 / 9.0) * ((stiff - 0.5) * here - beside)
            if k == 0:
                return here, 0.5 * twice
            return here, twice - table[k - 1][pl.ds(e, count)]

        def step(i, carry):
            squares, cross = carry
            e = FIELDS + i * stride
            packed = past_ref[k, pl.ds(1 + i * (stride // FIELDS), stride // FIELDS)]
            here, value = following(e, stride, slope_ref[pl.ds(i * stride, stride)], insertions(packed, 0, stride))
            if k < ITERS - 1:
                table[k + 1][pl.ds(e, stride)] = value
            return squares + jnp.sum(here * here, axis=0), cross + jnp.sum(here * value, axis=0)

        zero = jnp.zeros((levels, points), F32)
        sums.append(lax.fori_loop(0, rows // stride, step, (zero, zero)))
        if k < ITERS - 1:
            reach = ITERS - 1 - k
            table[k + 1][first - reach : first] = top * following(
                first - reach, reach, above_ref[FIELDS - reach : FIELDS, depth:],
                insertions(past_ref[k, 0:1], FIELDS - reach, reach),
            )[1]
            table[k + 1][last + 1 : last + 1 + reach] = bottom * following(
                last + 1, reach, below_ref[0:reach, depth:], insertions(past_ref[k, groups + 1 :], 0, reach)
            )[1]

    lane = lanes((1, points))
    moments = jnp.zeros((1, points), F32)
    for i, value in enumerate([a for a, _ in sums] + [b for _, b in sums]):
        total = jnp.sum(jnp.sum(value, axis=0, keepdims=True), axis=1, keepdims=True)
        moments = jnp.where(lane == i, total, moments)
    moments_ref[...] = jnp.broadcast_to(moments, moments_ref.shape)


def make_basis(info, above, below, begun, sides, stiffness, ends, smooth, polar, devices):
    rows, levels, points = stiffness.shape
    depth = 3 * levels
    groups = rows // FIELDS + 2
    both = depth + levels
    vmem = pl.BlockSpec(memory_space=pltpu.VMEM)
    return pl.pallas_call(
        basis_kernel,
        in_specs=[pl.BlockSpec(memory_space=pltpu.SMEM)] + [pl.BlockSpec(memory_space=pl.ANY)] * 5 + [vmem] * 2,
        out_specs=(vmem,) * (ITERS + 3),
        out_shape=(pltpu.VMEM((rows + 2 * FIELDS, levels, points), F32),) * ITERS
        + (
            pltpu.VMEM((ITERS, groups, levels, points), F32),
            pltpu.HBM((polar, depth, points), F32),
            jax.ShapeDtypeStruct((devices, points), F32),
        ),
        scratch_shapes=[
            pltpu.VMEM((2, groups, both, points), F32),
            pltpu.VMEM(stiffness.shape, F32),
            pltpu.VMEM((polar + 2, depth, points), F32),
            pltpu.VMEM((polar // FIELDS, levels, points), F32),
            pltpu.VMEM((ITERS, 2, groups, levels, points), F32),
            pltpu.VMEM((2, groups, levels, points), F32),
            pltpu.VMEM(above.shape, F32),
            pltpu.VMEM(below.shape, F32),
            pltpu.SemaphoreType.DMA((5,)),
        ],
        cost_estimate=pl.CostEstimate(flops=40000000, bytes_accessed=24000000, transcendentals=0),
        compiler_params=params(16),
        name="basis",
    )(info, above, below, *[in_hbm(x) for x in (begun, sides, stiffness)], ends, smooth)


def solve(mu):
    gram = [[0.5 * (mu[i + j] + mu[abs(i - j)]) for j in range(ITERS + 1)] for i in range(ITERS)]

    def inner(a, b):
        return tree([x * tree([y * gram[i][j] for j, y in enumerate(b)]) for i, x in enumerate(a)])

    def image_of(a):
        out = [4.5 * x for x in a] + [jnp.zeros_like(a[0])]
        for k, x in enumerate(a):
            out[k + 1] = out[k + 1] + 2.25 * x
            out[abs(k - 1)] = out[abs(k - 1)] + 2.25 * x
        return out

    zero = jnp.zeros_like(mu[0])
    phi = []
    residual = [zero + 1.0]
    direction = residual
    norm = mu[0]
    for step in range(ITERS):
        image = image_of(direction)
        alpha = norm / inner(direction, image)
        phi = [x + alpha * y for x, y in zip(phi + [zero], direction)]
        if step < ITERS - 1:
            residual = [x - alpha * y for x, y in zip(residual + [zero], image)]
            following = inner(residual, residual)
            ratio = following / norm
            direction = [x + ratio * y for x, y in zip(residual, direction + [zero])]
            norm = following
    return phi


def finish_kernel(
    info_ref, spread_ref, filtered_hbm, caps_hbm, t0, t1, t2, t3, t4, past_ref, out_ref,
    coefficient_ref, filtered_ref, caps_ref, sems,
):
    table = [t0, t1, t2, t3, t4]
    _, levels, points = t0.shape
    block = out_ref.shape[0]
    g = pl.program_id(0)

    def fetch(i):
        part = pl.ds(i * block, block)
        return pltpu.make_async_copy(filtered_hbm.at[part], filtered_ref.at[part], sems.at[i])

    polar = caps_ref.shape[0]
    start, is_polar = info_ref[0], info_ref[1]
    fetch_caps = pltpu.make_async_copy(caps_hbm, caps_ref, sems.at[filtered_ref.shape[0] // block])

    @pl.when(g == 0)
    def _():
        fetch_caps.start()
        for i in range(filtered_ref.shape[0] // block):
            fetch(i).start()
        total = jnp.sum(spread_ref[...], axis=0, keepdims=True)
        lane = lanes(total.shape)
        picked = [
            jnp.sum(jnp.where(lane == i, total, 0.0), axis=1, keepdims=True) for i in range(2 * ITERS)
        ]
        mu = [picked[0], picked[ITERS]]
        for k in range(1, ITERS):
            mu += [2.0 * picked[k] - mu[0], 2.0 * picked[ITERS + k] - mu[1]]
        for k, value in enumerate(solve(mu)):
            coefficient_ref[k] = jnp.broadcast_to(value, (8, points))

    c = [jnp.concatenate([coefficient_ref[k]] * (levels // 8), axis=0) for k in range(ITERS)]

    fetch(g).wait()

    @pl.when(g == 0)
    def _():
        fetch_caps.wait()

    @pl.when((is_polar == 1) & (g == start // block))
    def _():
        filtered_ref[pl.ds(start, polar)] = caps_ref[...]

    def phi_of(e):
        return tree([c[k] * table[k][e] for k in range(ITERS)])

    lane = lanes((levels, points))
    stride = FIELDS

    def step(i, carry):
        first = i * stride
        row = g * block + first
        near = list(carry) + [phi_of(FIELDS + row + 1 + j) for j in range(stride)]
        packed = tree([c[k] * past_ref[k, 1 + row // FIELDS] for k in range(ITERS)])
        old = [filtered_ref[row + j] for j in range(stride)]
        new = []
        for j in range(stride):
            here = near[j + 1]
            inserted = unpack_lanes(packed, j)
            east = jnp.where(lane == points - 1, inserted, shift(here, -1))
            west = jnp.where(lane == 0, inserted, shift(here, 1))
            new.append(old[j][0:levels] - 0.5 * (east - west))
            new.append(old[j][levels : 2 * levels] - 0.5 * (near[j + 2] - near[j]))
            new.append(old[j][2 * levels :] - here)
        for j in range(stride):
            for part in range(3):
                out_ref[first + j, part * levels : (part + 1) * levels] = new[3 * j + part]
        return near[stride], near[stride + 1]

    e = FIELDS + g * block
    lax.fori_loop(0, block // stride, step, (phi_of(e - 1), phi_of(e)), unroll=True)


def finish(info, spread, filtered, caps, table):
    rows, depth, points = filtered.shape
    block = 32
    vmem = pl.BlockSpec(memory_space=pltpu.VMEM)
    piece = pl.BlockSpec((block, depth, points), lambda g: (g, 0, 0))
    return pl.pallas_call(
        finish_kernel,
        grid=(rows // block,),
        in_specs=[pl.BlockSpec(memory_space=pltpu.SMEM), vmem] + [pl.BlockSpec(memory_space=pl.ANY)] * 2 + [vmem] * (ITERS + 1),
        out_specs=piece,
        out_shape=jax.ShapeDtypeStruct((rows, depth, points), F32),
        scratch_shapes=[
            pltpu.VMEM((ITERS, 8, points), F32),
            pltpu.VMEM((rows, depth, points), F32),
            pltpu.VMEM(caps.shape, F32),
            pltpu.SemaphoreType.DMA((rows // block + 1,)),
        ],
        cost_estimate=pl.CostEstimate(flops=20000000, bytes_accessed=17000000, transcendentals=0),
        compiler_params=params(12),
        name="finish",
    )(info, spread, in_hbm(filtered), in_hbm(caps), *table)


def shards(state, weights, owners, source_rows, cutoffs, stiffness):
    rows, comps, levels, points = state.shape
    depth = comps * levels
    n_lon = lax.axis_size("lon")
    n_lat = lax.axis_size("lat")
    devices = n_lon * n_lat
    band = lax.axis_index("lat")
    north, south = band == 0, band == n_lat - 1
    polar = cutoffs.shape[0] // 2
    line = lax.axis_index("lon") * polar // n_lon
    info = jnp.stack(
        [
            jnp.where(north, 0, rows - polar),
            (north | south).astype(jnp.int32),
            (band > 0).astype(jnp.int32),
            (band < n_lat - 1).astype(jnp.int32),
            cutoffs[jnp.where(north, line, polar + line)],
        ]
    ).astype(jnp.int32)

    requests, place = make_requests(owners[:, :, 0], source_rows)
    asked = exchange(requests, BOTH)[:, :2]
    asked, ahead, ahead_weights = lax.optimization_barrier((asked, stiffness, weights))
    moved = exchange(state[asked], BOTH).reshape(2 * devices, depth, points)
    moved, rim_weights, *stiff = lax.optimization_barrier(
        (moved, edge_weights(ahead_weights)) + tuple(pack_stiffness(ahead))
    )

    place = place[0]
    caps, last, first = make_caps(place, info, moved, weights, stiffness, polar)
    lines = exchange(caps.reshape(n_lon, -1, points), "lon")
    place, caps = lax.optimization_barrier((place, caps))
    to_east, to_west, own = make_edges(place, moved, rim_weights, stiff)
    west, east = from_sides(to_east, to_west)
    passed = low_pass(info, lines)
    smooth = exchange(passed, "lon")
    _, west_late, east_late = lax.optimization_barrier((passed, west, east))
    above, below = from_ends(*make_ends(last, first, west_late, east_late))
    arrived, begun, sides, near = prepare(place, info, moved, weights, west, east, own)
    *table, caps, moments = make_basis(info, above, below, begun, sides, stiffness, near, smooth, polar, devices)
    out = finish(info, exchange(moments, BOTH), arrived, caps, table)
    return out.reshape(rows, comps, levels, points)


def solution(mesh):
    in_specs = (
        P("lat", None, None, "lon"),
        P("lat", None, "lon"),
        P("lon", "lat", None),
        P("lon", "lat"),
        P(),
        P("lat", None, "lon"),
    )
    out_specs = P("lat", None, None, "lon")
    return jax.shard_map(shards, mesh=mesh, in_specs=in_specs, out_specs=out_specs, check_vma=False)
```
